512 devices in a mesh: lon: 32 (over z_lo, y, core), lat: 4 (over x), lev: 4 (over z_hi).
Axes of the slice: x: 4, y: 8, z: 8 (z_hi: 4, z_lo: 2; z = z_hi * 2 + z_lo), core: 2. Of those that a mesh axis runs over, the one named last changes fastest.
Arguments:
- bin_burden: float32 [9, 16, 32, 4096], P(None, 'lev', 'lat', 'lon'), may hold values from 0.05 to 5
- zonal_cfl_ratio: float32 [16, 32, 4096], P('lev', 'lat', 'lon'), may hold values from -0.24 to 0.24
- meridional_cfl_ratio: float32 [16, 32, 4096], P('lev', 'lat', 'lon'), may hold values from -0.24 to 0.24
- thermal_kelvins: float32 [16, 32, 4096], P('lev', 'lat', 'lon'), may hold values from 220 to 300
- diffusion_coefficient: float32 [16, 32, 4096], P('lev', 'lat', 'lon'), may hold values from 5 to 300
- inert_emitted_aerosol: float32 [16, 32, 4096], P('lev', 'lat', 'lon'), may hold values from 0.5 to 5
- heat_of_evaporation: float32 [9], replicated, may hold values from 50 to 150
- damped_parallels: int32 [8], replicated, may hold values from 0 to 31, as said below
- preserved_harmonic_limits: int32 [8], replicated, may hold values from 1 to 128, as said below
Outputs:
- condensed_mass: float32 [9, 16, 32, 4096], P(None, 'lev', 'lat', 'lon')
- gas_phase: float32 [9, 16, 32, 4096], P(None, 'lev', 'lat', 'lon')
The draws below stay inside these ranges and needn't reach their ends.
Inputs may be any that keep to these rules, and one draw needn't show every extreme that they name: `damped_parallels`: entries 0 to 3 are distinct rows below 8, entry 0 being row 0; entries 4 to 7 are distinct rows of at least 24, entry 4 being row 31. preserved_harmonic_limits[0] = 1 and preserved_harmonic_limits[1] = 128.
All inputs are finite; a program needn't handle non-finite values.
Results may differ from the reference program's by a relative error of at most 0.0003.
Values sent between devices are 32-bit elements; how exact they have to be, the bound alone decides.
No kernel may reach another device: no remote copies, remote signals or barrier semaphores. Data moves between devices by JAX's collectives and lax.ppermute only.
A program may use at most 64 MiB of HBM per device.

```python
import math
import jax
import jax.numpy as jnp
from jax import lax

BINS = 9
HEIGHT_LAYERS = 16
LAT_DEV = 8
POLE = 4
MMAX = 128
PITERS = 3
MERIDIAN_SIZE = 4096
PARALLEL_SIZE = 32


def draw_damped_parallels(key, part):
    north_others = jax.random.permutation(jax.random.fold_in(key, 11), LAT_DEV - 1)[:POLE - 1] + 1
    south_others = jax.random.permutation(jax.random.fold_in(key, 23), LAT_DEV - 1)[:POLE - 1] + 1
    northern = jnp.concatenate([jnp.zeros((1,), jnp.int32), north_others.astype(jnp.int32)])
    southern = PARALLEL_SIZE - 1 - jnp.concatenate([jnp.zeros((1,), jnp.int32), south_others.astype(jnp.int32)])
    return jnp.concatenate([northern, southern]).astype(jnp.int32)


def draw_preserved_harmonic_limits(key, part):
    counts = jax.random.randint(key, (2 * POLE,), 1, MMAX + 1)
    return counts.at[0].set(1).at[1].set(MMAX).astype(jnp.int32)


def block_levels(stream_key, dims, split, least, high):
    gain, own = 1.0, jax.random.fold_in(stream_key, 6)
    for dim, shards_of in split:
        heights = jnp.exp(jax.random.uniform(jax.random.fold_in(own, dim), (shards_of,), jnp.float32, least / len(split), high / len(split)))
        gain = gain * jnp.repeat(heights, dims[dim] // shards_of).reshape([-1 if axis == dim else 1 for axis in range(len(dims))])
    return gain


def setup_inputs(seed: int = 0) -> dict:
    key_of = jax.random.split(jax.random.key(seed), 10)
    bin_burden = jnp.clip(jnp.exp(math.log(5.0) - 4.6051702 * jax.random.uniform(key_of[0], (BINS, HEIGHT_LAYERS, PARALLEL_SIZE, MERIDIAN_SIZE), jnp.float32) ** block_levels(key_of[0], (BINS, HEIGHT_LAYERS, PARALLEL_SIZE, MERIDIAN_SIZE), ((1, 4), (2, 4), (3, 32)), -0.2, 0.2)), 0.05, 5.0)
    zonal_cfl_ratio = jnp.clip(jax.random.uniform(key_of[1], (HEIGHT_LAYERS, PARALLEL_SIZE, MERIDIAN_SIZE), jnp.float32, -0.24, 0.24) * block_levels(key_of[1], (HEIGHT_LAYERS, PARALLEL_SIZE, MERIDIAN_SIZE), ((0, 4), (1, 4), (2, 32)), -0.4, 0.0), -0.24, 0.24)
    meridional_cfl_ratio = jnp.clip(jax.random.uniform(key_of[2], (HEIGHT_LAYERS, PARALLEL_SIZE, MERIDIAN_SIZE), jnp.float32, -0.24, 0.24) * block_levels(key_of[2], (HEIGHT_LAYERS, PARALLEL_SIZE, MERIDIAN_SIZE), ((0, 4), (1, 4), (2, 32)), -0.4, 0.0), -0.24, 0.24)
    thermal_kelvins = jnp.clip(220.0 + 80.0 * jax.random.uniform(key_of[3], (HEIGHT_LAYERS, PARALLEL_SIZE, MERIDIAN_SIZE), jnp.float32) ** block_levels(key_of[3], (HEIGHT_LAYERS, PARALLEL_SIZE, MERIDIAN_SIZE), ((0, 4), (1, 4), (2, 32)), -0.2, 0.2), 220.0, 300.0)
    diffusion_coefficient = jnp.clip(jnp.exp(math.log(300.0) - 4.0943446 * jax.random.uniform(key_of[4], (HEIGHT_LAYERS, PARALLEL_SIZE, MERIDIAN_SIZE), jnp.float32) ** block_levels(key_of[4], (HEIGHT_LAYERS, PARALLEL_SIZE, MERIDIAN_SIZE), ((0, 4), (1, 4), (2, 32)), -0.2, 0.2)), 5.0, 300.0)
    inert_emitted_aerosol = jnp.clip(jnp.exp(math.log(5.0) - 2.3025851 * jax.random.uniform(key_of[5], (HEIGHT_LAYERS, PARALLEL_SIZE, MERIDIAN_SIZE), jnp.float32) ** block_levels(key_of[5], (HEIGHT_LAYERS, PARALLEL_SIZE, MERIDIAN_SIZE), ((0, 4), (1, 4), (2, 32)), -0.2, 0.2)), 0.5, 5.0)
    heat_of_evaporation = jnp.clip(jax.random.uniform(key_of[6], (BINS,), jnp.float32, 50.0, 150.0), 50.0, 150.0)
    damped_parallels = draw_damped_parallels(jax.random.fold_in(key_of[9], 71), 0)
    preserved_harmonic_limits = draw_preserved_harmonic_limits(jax.random.fold_in(key_of[9], 71), 0)
    return dict(bin_burden=bin_burden, zonal_cfl_ratio=zonal_cfl_ratio, meridional_cfl_ratio=meridional_cfl_ratio, thermal_kelvins=thermal_kelvins, diffusion_coefficient=diffusion_coefficient, inert_emitted_aerosol=inert_emitted_aerosol, heat_of_evaporation=heat_of_evaporation, damped_parallels=damped_parallels, preserved_harmonic_limits=preserved_harmonic_limits)


GAS_CONST = 8.314e-3
REF_TEMP = 298.0
LOG_TEN = 2.302585092994046
PRECISE = lax.Precision.HIGHEST


def effective_vapour_threshold(temper, heat_of_evaporation):
    bin_count = heat_of_evaporation.shape[0]
    decade = jnp.arange(bin_count).astype(jnp.float32) - 2.0
    shape_full = (bin_count,) + (1,) * temper.ndim
    base_value = jnp.exp(LOG_TEN * decade).reshape(shape_full)
    return base_value * (REF_TEMP / temper) * jnp.exp(heat_of_evaporation.reshape(shape_full) / GAS_CONST * (1.0 / REF_TEMP - 1.0 / temper))


def gas_condensed_partition(vertical_sums, temper, inert_emitted_aerosol, heat_of_evaporation):
    cstar = effective_vapour_threshold(temper, heat_of_evaporation)
    carbon_compounds = inert_emitted_aerosol
    for sweep_index in range(PITERS):
        carbon_compounds = inert_emitted_aerosol + jnp.sum(vertical_sums / (1.0 + cstar / carbon_compounds), axis=0)
    return carbon_compounds


def diffuse(amounts, diffusion_coefficient):
    level_count = diffusion_coefficient.shape[0]
    zeros_row = jnp.zeros_like(diffusion_coefficient[0])
    coupling = [zeros_row] + [diffusion_coefficient[k] for k in range(1, level_count)] + [zeros_row]
    sweep_upper = []
    sweep_source = []
    for k in range(level_count):
        below_term = -coupling[k]
        above_term = -coupling[k + 1]
        centre_term = 1.0 + coupling[k] + coupling[k + 1]
        if k == 0:
            pivot_value = centre_term
            source_term = amounts[:, 0]
        else:
            pivot_value = centre_term - below_term * sweep_upper[k - 1]
            source_term = amounts[:, k] - below_term * sweep_source[k - 1]
        sweep_upper.append(above_term / pivot_value)
        sweep_source.append(source_term / pivot_value)
    solved = [sweep_source[-1]]
    for k in range(level_count - 2, -1, -1):
        solved.insert(0, sweep_source[k] - sweep_upper[k] * solved[0])
    return jnp.stack(solved, axis=1)


def tables(columns, wavenumber, circle):
    phase_angle = ((columns[:, None] * wavenumber[None, :]) % circle).astype(jnp.float32) * (2.0 * math.pi / circle)
    return jnp.cos(phase_angle), jnp.sin(phase_angle)


def advect(bin_burden, zonal_cfl_ratio, meridional_cfl_ratio):
    row_count = bin_burden.shape[2]
    open_rows = (jnp.arange(row_count) > 0).astype(bin_burden.dtype)
    south_faces = meridional_cfl_ratio * open_rows[None, :, None]
    north_faces = jnp.concatenate([south_faces[:, 1:], jnp.zeros_like(south_faces[:, :1])], axis=1)
    east_faces = jnp.roll(zonal_cfl_ratio, -1, axis=2)
    west_cells = jnp.roll(bin_burden, 1, axis=3)
    east_cells = jnp.roll(bin_burden, -1, axis=3)
    south_cells = jnp.concatenate([jnp.zeros_like(bin_burden[:, :, :1]), bin_burden[:, :, :-1]], axis=2)
    north_cells = jnp.concatenate([bin_burden[:, :, 1:], jnp.zeros_like(bin_burden[:, :, :1])], axis=2)
    flux_west = jnp.maximum(zonal_cfl_ratio, 0.0) * west_cells + jnp.minimum(zonal_cfl_ratio, 0.0) * bin_burden
    flux_east = jnp.maximum(east_faces, 0.0) * bin_burden + jnp.minimum(east_faces, 0.0) * east_cells
    flux_south = jnp.maximum(south_faces, 0.0) * south_cells + jnp.minimum(south_faces, 0.0) * bin_burden
    flux_north = jnp.maximum(north_faces, 0.0) * bin_burden + jnp.minimum(north_faces, 0.0) * north_cells
    return bin_burden + flux_west - flux_east + flux_south - flux_north


def reference(bin_burden, zonal_cfl_ratio, meridional_cfl_ratio, thermal_kelvins, diffusion_coefficient, inert_emitted_aerosol, heat_of_evaporation, damped_parallels, preserved_harmonic_limits):
    advected = advect(bin_burden, zonal_cfl_ratio, meridional_cfl_ratio)
    circle = advected.shape[3]
    wavenumber = jnp.arange(MMAX).astype(jnp.int32)
    cosine, sine = tables(jnp.arange(circle).astype(jnp.int32), wavenumber, circle)
    selected = advected[:, :, damped_parallels, :]
    cosine_part = jnp.einsum("bkpi,im->bkpm", selected, cosine, precision=PRECISE)
    sine_part = jnp.einsum("bkpi,im->bkpm", selected, sine, precision=PRECISE)
    weight = jnp.where(wavenumber[None, :] < preserved_harmonic_limits[:, None], jnp.where(wavenumber[None, :] == 0, 1.0, 2.0), 0.0).astype(jnp.float32)
    smooth = (jnp.einsum("bkpm,im->bkpi", cosine_part * weight, cosine, precision=PRECISE) + jnp.einsum("bkpm,im->bkpi", sine_part * weight, sine, precision=PRECISE)) / circle
    damped_parallel_fields = advected.at[:, :, damped_parallels, :].set(smooth)
    vertical_sums = diffuse(damped_parallel_fields, diffusion_coefficient)
    carbon_compounds = gas_condensed_partition(vertical_sums, thermal_kelvins, inert_emitted_aerosol, heat_of_evaporation)
    condensed_mass = vertical_sums / (1.0 + effective_vapour_threshold(thermal_kelvins, heat_of_evaporation) / carbon_compounds)
    return condensed_mass, vertical_sums - condensed_mass
```

```python
import math

import jax
import jax.numpy as jnp
import numpy as np
from jax import lax
from jax.experimental import pallas as pl
from jax.experimental.pallas import tpu as pltpu
from jax.sharding import PartitionSpec as P

BINS = 9
LEVELS = 4
TILES = BINS * LEVELS
ROWS = 8
WIDTH = 128
RING = 32
POLE = 4
CIRCLES = POLE * TILES
SHARE = 5
MODES = 128
CIRCLE = RING * WIDTH
PITERS = 3
GAS_CONST = 0.008314
REF_TEMP = 298.0
PRECISE = lax.Precision.HIGHEST
F32 = jnp.float32
VMEM = pl.BlockSpec(memory_space=pltpu.VMEM)
SMEM = pl.BlockSpec(memory_space=pltpu.SMEM)
GROUP = 40


def shape(*dims):
    return jax.ShapeDtypeStruct(dims, F32)


def call(kernel, name, outs, in_specs):
    return pl.pallas_call(
        kernel,
        out_shape=outs,
        in_specs=in_specs,
        out_specs=tuple(VMEM for _ in outs),
        compiler_params=pltpu.CompilerParams(vmem_limit_bytes=16 * 2**20),
        name=name,
    )


def tables():
    modes = np.arange(MODES)

    def pair(columns):
        angle = (columns[:, None] * modes[None, :] % CIRCLE) * (2.0 * math.pi / CIRCLE)
        return np.cos(angle), np.sin(angle)

    inner = np.stack(pair(np.arange(WIDTH))).astype(np.float32)
    first = pair(np.arange(RING) * WIDTH)
    before = pair(np.arange(RING) * WIDTH - 1)
    outer = np.stack([first[0], first[1], first[0] - before[0], first[1] - before[1]])
    return jnp.asarray(inner), jnp.asarray(outer.astype(np.float32))


def iotas():
    lane = lax.broadcasted_iota(jnp.int32, (ROWS, WIDTH), 1)
    row = lax.broadcasted_iota(jnp.int32, (ROWS, WIDTH), 0)
    return lane, row


def spread(row_vector):
    return jnp.broadcast_to(row_vector, (ROWS, WIDTH))


def column(tile, at):
    return jnp.broadcast_to(tile[:, at : at + 1], (ROWS, WIDTH))


def chosen_rows(rows_ref):
    southern = lax.axis_index("lat") >= 2
    return [
        jnp.clip(
            jnp.where(southern, rows_ref[POLE + p] - 3 * ROWS, rows_ref[p]), 0, ROWS - 1
        )
        for p in range(POLE)
    ]


def edge_kernel(burden, merid, out_a, out_b):
    even = lax.axis_index("lat") % 2 == 0
    row_a = jnp.where(even, ROWS - 1, 0)
    row_b = ROWS - 1 - row_a
    for t in range(TILES):
        out_a[t : t + 1, :] = burden[t, pl.ds(row_a, 1), :]
        out_b[t : t + 1, :] = burden[t, pl.ds(row_b, 1), :]
    for k in range(LEVELS):
        at = TILES + k
        out_a[at : at + 1, :] = merid[k, pl.ds(row_a, 1), :]
        out_b[at : at + 1, :] = merid[k, pl.ds(row_b, 1), :]


def squeeze_rows(tile, lane):
    packed = jnp.zeros_like(tile)
    for g in range(3):
        moved = pltpu.roll(tile, (5 - 3 * g) % ROWS, 0)
        if g:
            moved = pltpu.roll(moved, GROUP * g, 1)
        packed = jnp.where((lane >= GROUP * g) & (lane < GROUP * (g + 1)), moved, packed)
    return packed


def unsqueeze_rows(packed, row):
    tile = jnp.zeros_like(packed)
    for g in range(3):
        moved = pltpu.roll(packed, (3 * g - 5) % ROWS, 0)
        if g:
            moved = pltpu.roll(moved, WIDTH - GROUP * g, 1)
        tile = jnp.where((row >= 3 * g) & (row < 3 * g + 3), moved, tile)
    return tile


def advect_kernel(rows_ref, burden, zonal, merid, halo_a, halo_b, partial, sent, edges, packs):
    lane, row = iotas()
    lat = lax.axis_index("lat")
    even = lat % 2 == 0
    first_row = (row == 0) & (lat == 0)
    west_edge = jnp.zeros((ROWS, WIDTH), F32)
    east_edge = jnp.zeros((ROWS, WIDTH), F32)
    face_edge = jnp.zeros((ROWS, WIDTH), F32)
    for k in range(LEVELS):
        face = zonal[k]
        inner = jnp.where(lane == 0, 0.0, face)
        up, down = jnp.maximum(inner, 0.0), jnp.minimum(inner, 0.0)
        south = jnp.where(first_row, 0.0, merid[k])
        south_up, south_down = jnp.maximum(south, 0.0), jnp.minimum(south, 0.0)
        at = TILES + k
        north = spread(jnp.where(even, halo_a[at : at + 1, :], halo_b[at : at + 1, :]))
        north_up, north_down = jnp.maximum(north, 0.0), jnp.minimum(north, 0.0)
        face_edge = jnp.where((lane < TILES) & (lane % LEVELS == k), column(face, 0), face_edge)
        for b in range(BINS):
            t = b * LEVELS + k
            tile = burden[t]
            row_a, row_b = halo_a[t : t + 1, :], halo_b[t : t + 1, :]
            below, above = jnp.where(even, row_b, row_a), jnp.where(even, row_a, row_b)
            west = up * pltpu.roll(tile, 1, 1) + down * tile
            below_cells = jnp.where(row == 0, spread(below), pltpu.roll(tile, 1, 0))
            from_south = south_up * below_cells + south_down * tile
            to_north = jnp.where(
                row == ROWS - 1,
                north_up * tile + north_down * spread(above),
                pltpu.roll(from_south, ROWS - 1, 0),
            )
            partial[t] = (
                tile + west - pltpu.roll(west, WIDTH - 1, 1) + from_south - to_north
            )
            west_edge = jnp.where(lane == t, column(tile, 0), west_edge)
            east_edge = jnp.where(lane == t, column(tile, WIDTH - 1), east_edge)
    edges[0] = east_edge
    edges[1] = west_edge
    edges[2] = face_edge
    packs[0] = squeeze_rows(east_edge, lane)
    packs[1] = squeeze_rows(
        jnp.where(lane < TILES, west_edge, pltpu.roll(face_edge, TILES, 1)), lane
    )
    rows = chosen_rows(rows_ref)
    low = jnp.zeros((ROWS, WIDTH), F32)
    high = jnp.zeros((ROWS, WIDTH), F32)
    for p in range(POLE):
        picked = [edges[e, pl.ds(rows[p], 1), :] for e in range(3)]
        tile = jnp.where(row == 5, spread(picked[0]), jnp.where(row == 6, spread(picked[1]), spread(picked[2])))
        start = TILES * p
        moved = pltpu.roll(tile, start, 1) if start else tile
        low = jnp.where((lane >= start) & (lane < start + TILES), moved, low)
        if start + TILES > 100:
            moved = pltpu.roll(tile, (start - 100) % WIDTH, 1)
            high = jnp.where((lane >= start - 100) & (lane < start - 100 + TILES), moved, high)
    for j in range(RING):
        start = SHARE * j
        source, offset = (low, start) if start + SHARE <= WIDTH else (high, start - 100)
        moved = pltpu.roll(source, (WIDTH - offset) % WIDTH, 1) if offset else source
        sent[j, SHARE:, :] = moved[SHARE:]
        for i in range(SHARE):
            n = start + i
            if n < CIRCLES:
                sent[j, i : i + 1, :] = partial[n % TILES, pl.ds(rows[n // TILES], 1), :]
            else:
                sent[j, i : i + 1, :] = jnp.zeros((1, WIDTH), F32)


def filter_kernel(limits_ref, received, packs, inner, outer, returned, parts):
    lane, row = iotas()
    me = lax.axis_index("lon")
    southern = lax.axis_index("lat") >= 2
    block = received[...]
    cosine, sine = inner[0], inner[1]
    flat = block.reshape(RING * ROWS, WIDTH)
    parts[...] = jnp.dot(
        flat,
        jnp.concatenate([cosine, sine], axis=1),
        precision=PRECISE,
        preferred_element_type=F32,
    )
    cosine_part = jnp.zeros((ROWS, MODES), F32)
    sine_part = jnp.zeros((ROWS, MODES), F32)
    for q in range(RING):
        c, s = outer[0, q : q + 1, :], outer[1, q : q + 1, :]
        own_c = parts[ROWS * q : ROWS * (q + 1), :MODES]
        own_s = parts[ROWS * q : ROWS * (q + 1), MODES:]
        cosine_part += c * own_c - s * own_s
        sine_part += s * own_c + c * own_s
    east_cells = received[:, 5, :]
    west_cells = received[:, 6, :]
    faces = received[:, 7, :]
    beyond = pltpu.roll(east_cells, 1, 0)
    flux = jnp.maximum(faces, 0.0) * beyond + jnp.minimum(faces, 0.0) * west_cells
    flux_lane = lax.broadcasted_iota(jnp.int32, flux.shape, 1)
    flux = jnp.where(flux_lane < SHARE, flux, 0.0)
    edge = lax.dot_general(
        flux,
        jnp.concatenate([outer[2], outer[3]], axis=1),
        (((0,), (0,)), ((), ())),
        precision=PRECISE,
        preferred_element_type=F32,
    )
    cosine_part += edge[:ROWS, :MODES]
    sine_part += edge[:ROWS, MODES:]
    limit = jnp.zeros((ROWS, MODES), jnp.int32)
    for i in range(SHARE):
        p = jnp.minimum((me * SHARE + i) // TILES, POLE - 1)
        kept = limits_ref[p + jnp.where(southern, POLE, 0)]
        limit = jnp.where(row == i, kept, limit)
    weight = jnp.where(lane < limit, jnp.where(lane == 0, 1.0, 2.0), 0.0) * (1.0 / CIRCLE)
    cosine_part *= weight
    sine_part *= weight
    for q in range(RING):
        c, s = outer[0, q : q + 1, :], outer[1, q : q + 1, :]
        parts[ROWS * q : ROWS * (q + 1), :MODES] = cosine_part * c + sine_part * s
        parts[ROWS * q : ROWS * (q + 1), MODES:] = sine_part * c - cosine_part * s
    smooth = jnp.dot(
        parts[...],
        jnp.concatenate([cosine, sine], axis=0),
        precision=PRECISE,
        preferred_element_type=F32,
    )
    returned[...] = smooth.reshape(RING, ROWS, WIDTH)
    returned[(me + 1) % RING, SHARE:, :] = packs[0, SHARE:, :]
    returned[(me + RING - 1) % RING, SHARE:, :] = packs[1, SHARE:, :]


def column_kernel(rows_ref, partial, edges, back, diffusion, local, response, payload, filtered):
    lane, row = iotas()
    me = lax.axis_index("lon")
    lat = lax.axis_index("lat")
    east_own, west_own, face_own = edges[0], edges[1], edges[2]
    from_west = unsqueeze_rows(back[(me + RING - 1) % RING], row)
    from_east = unsqueeze_rows(back[(me + 1) % RING], row)
    four = jnp.where(lane < LEVELS, pltpu.roll(from_east, WIDTH - TILES, 1), 0.0)
    eight = four + pltpu.roll(four, 4, 1)
    sixteen = eight + pltpu.roll(eight, 8, 1)
    face_next = sixteen + pltpu.roll(sixteen, 16, 1) + pltpu.roll(four, 32, 1)
    flux_in = jnp.maximum(face_own, 0.0) * from_west + jnp.minimum(face_own, 0.0) * west_own
    flux_out = jnp.maximum(face_next, 0.0) * east_own + jnp.minimum(face_next, 0.0) * from_east
    for t in range(TILES):
        filtered[t] = (
            partial[t]
            + jnp.where(lane == 0, column(flux_in, t), 0.0)
            - jnp.where(lane == WIDTH - 1, column(flux_out, t), 0.0)
        )
    rows = chosen_rows(rows_ref)

    @pl.when((lat == 0) | (lat == 3))
    def _():
        for n in range(CIRCLES):
            filtered[n % TILES, pl.ds(rows[n // TILES], 1), :] = back[n // SHARE, n % SHARE : n % SHARE + 1, :]

    a1, a2, a3 = diffusion[1], diffusion[2], diffusion[3]
    i0 = 1.0 / (1.0 + a1)
    w1 = a1 * i0
    e1 = 1.0 + w1
    i1 = 1.0 / (e1 + a2)
    w2 = a2 * i1
    e2 = 1.0 + w2 * e1
    i2 = 1.0 / (e2 + a3)
    w3 = a3 * i2
    i3 = 1.0 / (1.0 + w3 * e2)
    up3 = i3
    up2 = w3 * up3
    up1 = w2 * up2
    up0 = w1 * up1
    d1 = w1
    d2 = w2 * d1
    d3 = w3 * d2
    low3 = d3 * i3
    low2 = d2 * i2 + w3 * low3
    low1 = d1 * i1 + w2 * low2
    low0 = i0 + w1 * low1
    for at, value in enumerate((low0, low1, low2, low3, up0, up1, up2, up3)):
        response[at] = value
    for b in range(BINS):
        f0 = filtered[b * LEVELS]
        f1 = filtered[b * LEVELS + 1] + w1 * f0
        f2 = filtered[b * LEVELS + 2] + w2 * f1
        f3 = filtered[b * LEVELS + 3] + w3 * f2
        x3 = f3 * i3
        x2 = f2 * i2 + w3 * x3
        x1 = f1 * i1 + w2 * x2
        x0 = f0 * i0 + w1 * x1
        local[b * LEVELS] = x0
        local[b * LEVELS + 1] = x1
        local[b * LEVELS + 2] = x2
        local[b * LEVELS + 3] = x3
        payload[b] = x0
        payload[BINS + b] = x3
    payload[2 * BINS] = low0
    payload[2 * BINS + 1] = up3
    payload[2 * BINS + 2] = up0
    payload[2 * BINS + 3] = 1.0 / diffusion[0]


def pair_kernel(own, other, payload, inside):
    lev = lax.axis_index("lev")
    lower = lev % 2 == 0
    bottom = lev < 2

    def of_lower(at):
        return jnp.where(lower, own[at], other[at])

    def of_upper(at):
        return jnp.where(lower, other[at], own[at])

    scale = 1.0 / (of_upper(2 * BINS + 3) + of_lower(2 * BINS + 1) + of_upper(2 * BINS))
    through = jnp.where(bottom, of_upper(2 * BINS + 2), of_lower(2 * BINS + 2))
    coupling = through * scale
    facing = jnp.where(bottom, of_upper(2 * BINS + 1), of_lower(2 * BINS))
    sign = jnp.where(bottom, 1.0, -1.0)
    signed = through * sign
    inside[BINS] = coupling
    payload[BINS] = facing - through * coupling
    payload[BINS + 1] = jnp.where(bottom, 0.0, of_lower(2 * BINS + 3))
    for b in range(BINS):
        flux = (of_lower(BINS + b) - of_upper(b)) * scale
        inside[b] = flux
        payload[b] = jnp.where(bottom, of_upper(BINS + b), of_lower(b)) + signed * flux


def phase_kernel(heat, own, other, inside, local, response, kelvins, inert, condensed, gas):
    lev = lax.axis_index("lev")
    lower = lev % 2 == 0
    middle = (lev == 1) | (lev == 2)
    sign = jnp.where(lev < 2, 1.0, -1.0)
    scale = sign / (own[BINS + 1] + other[BINS + 1] + own[BINS] + other[BINS])
    below, above = [], []
    for b in range(BINS):
        centre = (own[b] - other[b]) * scale
        mid = inside[b] + inside[BINS] * centre
        open_end = jnp.where(middle, centre, 0.0)
        below.append(jnp.where(lower, open_end, mid))
        above.append(jnp.where(lower, mid, open_end))
    for k in range(LEVELS):
        inverse = 1.0 / kelvins[k]
        ratio = REF_TEMP * inverse
        slope = (1.0 / REF_TEMP - inverse) * (1.0 / GAS_CONST)
        low, up = response[k], response[LEVELS + k]
        emitted = inert[k]
        totals, threshold = [], []
        for b in range(BINS):
            totals.append(local[b * LEVELS + k] + low * below[b] - up * above[b])
            threshold.append((10.0 ** (b - 2)) * ratio * jnp.exp(heat[b] * slope))
        organic = emitted
        for _ in range(PITERS):
            held = emitted
            for b in range(BINS):
                held = held + totals[b] * (organic / (organic + threshold[b]))
            organic = held
        for b in range(BINS):
            particle = totals[b] * (organic / (organic + threshold[b]))
            condensed[b * LEVELS + k] = particle
            gas[b * LEVELS + k] = totals[b] - particle


def body(
    bin_burden,
    zonal_cfl_ratio,
    meridional_cfl_ratio,
    thermal_kelvins,
    diffusion_coefficient,
    inert_emitted_aerosol,
    heat_of_evaporation,
    damped_parallels,
    preserved_harmonic_limits,
):
    burden = bin_burden.reshape(TILES, ROWS, WIDTH)
    inner, outer = tables()
    field = shape(TILES, ROWS, WIDTH)
    out_a, out_b = call(
        edge_kernel, "edge", (shape(GROUP, WIDTH), shape(GROUP, WIDTH)), [VMEM] * 2
    )(burden, meridional_cfl_ratio)
    halo_a = lax.ppermute(out_a, "lat", [(0, 1), (1, 0), (2, 3), (3, 2)])
    halo_b = lax.ppermute(out_b, "lat", [(1, 2), (2, 1)])
    partial, sent, edges, packs = call(
        advect_kernel,
        "advect",
        (field, shape(RING, ROWS, WIDTH), shape(3, ROWS, WIDTH), shape(2, ROWS, WIDTH)),
        [SMEM] + [VMEM] * 5,
    )(damped_parallels, burden, zonal_cfl_ratio, meridional_cfl_ratio, halo_a, halo_b)
    received = lax.all_to_all(sent, "lon", 0, 0, tiled=True)
    returned, _ = call(
        filter_kernel,
        "filter",
        (shape(RING, ROWS, WIDTH), shape(RING * ROWS, 2 * MODES)),
        [SMEM] + [VMEM] * 4,
    )(preserved_harmonic_limits, received, packs, inner, outer)
    back = lax.all_to_all(returned, "lon", 0, 0, tiled=True)
    ends = shape(2 * BINS + 4, ROWS, WIDTH)
    local, response, payload, _ = call(
        column_kernel,
        "column",
        (field, shape(2 * LEVELS, ROWS, WIDTH), ends, field),
        [SMEM] + [VMEM] * 4,
    )(damped_parallels, partial, edges, back, diffusion_coefficient)
    partner = lax.ppermute(payload, "lev", [(0, 1), (1, 0), (2, 3), (3, 2)])
    facing, inside = call(
        pair_kernel,
        "pair",
        (shape(BINS + 2, ROWS, WIDTH), shape(BINS + 1, ROWS, WIDTH)),
        [VMEM] * 2,
    )(payload, partner)
    across = lax.ppermute(facing, "lev", [(0, 3), (3, 0), (1, 2), (2, 1)])
    condensed, gas = call(phase_kernel, "phase", (field, field), [SMEM] + [VMEM] * 7)(
        heat_of_evaporation,
        facing,
        across,
        inside,
        local,
        response,
        thermal_kelvins,
        inert_emitted_aerosol,
    )
    return condensed.reshape(bin_burden.shape), gas.reshape(bin_burden.shape)


def solution(mesh):
    block = P("lev", "lat", "lon")
    binned = P(None, "lev", "lat", "lon")
    return jax.shard_map(
        body,
        mesh=mesh,
        in_specs=(binned, block, block, block, block, block, P(), P(), P()),
        out_specs=(binned, binned),
        check_vma=False,
    )
```

```python
import math

import jax
import jax.numpy as jnp
import numpy as np
from jax import lax
from jax.experimental import pallas as pl
from jax.experimental.pallas import tpu as pltpu
from jax.sharding import PartitionSpec as P

BINS = 9
LEVELS = 4
TILES = BINS * LEVELS
ROWS = 8
WIDTH = 128
RING = 32
POLE = 4
CIRCLES = POLE * TILES
SHARE = 5
MODES = 128
CIRCLE = RING * WIDTH
PITERS = 3
GAS_CONST = 0.008314
REF_TEMP = 298.0
PRECISE = lax.Precision.HIGHEST
F32 = jnp.float32
VMEM = pl.BlockSpec(memory_space=pltpu.VMEM)
SMEM = pl.BlockSpec(memory_space=pltpu.SMEM)
HBM = pl.BlockSpec(memory_space=pltpu.HBM)
GROUP = 40


def shape(*dims):
    return jax.ShapeDtypeStruct(dims, F32)


def call(kernel, name, outs, in_specs, scratch=()):
    return pl.pallas_call(
        kernel,
        out_shape=outs,
        in_specs=in_specs,
        out_specs=tuple(VMEM for _ in outs),
        scratch_shapes=list(scratch),
        compiler_params=pltpu.CompilerParams(vmem_limit_bytes=16 * 2**20),
        name=name,
    )


def tables():
    modes = np.arange(MODES)

    def pair(columns):
        angle = (columns[:, None] * modes[None, :] % CIRCLE) * (2.0 * math.pi / CIRCLE)
        return np.cos(angle), np.sin(angle)

    inner = np.stack(pair(np.arange(WIDTH))).astype(np.float32)
    first = pair(np.arange(RING) * WIDTH)
    before = pair(np.arange(RING) * WIDTH - 1)
    outer = np.stack([first[0], first[1], first[0] - before[0], first[1] - before[1]])
    return jnp.asarray(inner), jnp.asarray(outer.astype(np.float32))


def iotas():
    lane = lax.broadcasted_iota(jnp.int32, (ROWS, WIDTH), 1)
    row = lax.broadcasted_iota(jnp.int32, (ROWS, WIDTH), 0)
    return lane, row


def spread(row_vector):
    return jnp.broadcast_to(row_vector, (ROWS, WIDTH))


def column(tile, at):
    return jnp.broadcast_to(tile[:, at : at + 1], (ROWS, WIDTH))


def chosen_rows(rows_ref):
    southern = lax.axis_index("lat") >= 2
    return [
        jnp.clip(
            jnp.where(southern, rows_ref[POLE + p] - 3 * ROWS, rows_ref[p]), 0, ROWS - 1
        )
        for p in range(POLE)
    ]


def edge_kernel(burden, merid, out_a, out_b, sems):
    even = lax.axis_index("lat") % 2 == 0
    row_a = jnp.where(even, ROWS - 1, 0)
    row_b = ROWS - 1 - row_a
    copies = []
    for at, (out, row) in enumerate(((out_a, row_a), (out_b, row_b))):
        for half, (source, start, count) in enumerate(((burden, 0, TILES), (merid, TILES, LEVELS))):
            copies.append(
                pltpu.make_async_copy(
                    source.at[:, pl.ds(row, 1), :],
                    out.at[start : start + count],
                    sems.at[2 * at + half],
                )
            )
    for copy in copies:
        copy.start()
    for copy in copies:
        copy.wait()


def setup_kernel(rows_ref, limits_ref, heat, kelvins, weight, code, threshold):
    lane, row = iotas()
    me = lax.axis_index("lon")
    lat = lax.axis_index("lat")
    southern = lat >= 2
    limit = jnp.zeros((ROWS, MODES), jnp.int32)
    for i in range(SHARE):
        p = jnp.minimum((me * SHARE + i) // TILES, POLE - 1)
        kept = limits_ref[p + jnp.where(southern, POLE, 0)]
        limit = jnp.where(row == i, kept, limit)
    weight[...] = jnp.where(lane < limit, jnp.where(lane == 0, 1.0, 2.0), 0.0) * (1.0 / CIRCLE)
    active = (lat == 0) | (lat == 3)
    slot = jnp.full((ROWS, WIDTH), -1, jnp.int32)
    for p, at in enumerate(chosen_rows(rows_ref)):
        slot = jnp.where((row == at) & active, p, slot)
    code[...] = slot
    for k in range(LEVELS):
        inverse = 1.0 / kelvins[k]
        ratio = REF_TEMP * inverse
        slope = (1.0 / REF_TEMP - inverse) * (1.0 / GAS_CONST)
        for b in range(BINS):
            threshold[b * LEVELS + k] = (10.0 ** (b - 2)) * ratio * jnp.exp(heat[b] * slope)


def squeeze_rows(tile, lane):
    packed = jnp.zeros_like(tile)
    for g in range(3):
        moved = pltpu.roll(tile, (5 - 3 * g) % ROWS, 0)
        if g:
            moved = pltpu.roll(moved, GROUP * g, 1)
        packed = jnp.where((lane >= GROUP * g) & (lane < GROUP * (g + 1)), moved, packed)
    return packed


def unsqueeze_rows(packed, row):
    tile = jnp.zeros_like(packed)
    for g in range(3):
        moved = pltpu.roll(packed, (3 * g - 5) % ROWS, 0)
        if g:
            moved = pltpu.roll(moved, WIDTH - GROUP * g, 1)
        tile = jnp.where((row >= 3 * g) & (row < 3 * g + 3), moved, tile)
    return tile


def advect_kernel(rows_ref, burden, zonal, merid, halo_a, partial, sent, edges, packs):
    lane, row = iotas()
    lat = lax.axis_index("lat")
    even = lat % 2 == 0
    first_row = (row == 0) & (lat == 0)
    west_edge = jnp.zeros((ROWS, WIDTH), F32)
    east_edge = jnp.zeros((ROWS, WIDTH), F32)
    face_edge = jnp.zeros((ROWS, WIDTH), F32)
    for k in range(LEVELS):
        face = zonal[k]
        inner = jnp.where(lane == 0, 0.0, face)
        up, down = jnp.maximum(inner, 0.0), jnp.minimum(inner, 0.0)
        south = jnp.where(first_row, 0.0, merid[k])
        south_up, south_down = jnp.maximum(south, 0.0), jnp.minimum(south, 0.0)
        north = spread(jnp.where(even, halo_a[TILES + k], 0.0))
        north_up, north_down = jnp.maximum(north, 0.0), jnp.minimum(north, 0.0)
        face_edge = jnp.where((lane < TILES) & (lane % LEVELS == k), column(face, 0), face_edge)
        for b in range(BINS):
            t = b * LEVELS + k
            tile = burden[t]
            beside = halo_a[t]
            below, above = jnp.where(even, 0.0, beside), jnp.where(even, beside, 0.0)
            west = up * pltpu.roll(tile, 1, 1) + down * tile
            below_cells = jnp.where(row == 0, spread(below), pltpu.roll(tile, 1, 0))
            from_south = south_up * below_cells + south_down * tile
            to_north = jnp.where(
                row == ROWS - 1,
                north_up * tile + north_down * spread(above),
                pltpu.roll(from_south, ROWS - 1, 0),
            )
            partial[t] = (
                tile + west - pltpu.roll(west, WIDTH - 1, 1) + from_south - to_north
            )
            west_edge = jnp.where(lane == t, column(tile, 0), west_edge)
            east_edge = jnp.where(lane == t, column(tile, WIDTH - 1), east_edge)
    edges[0] = east_edge
    edges[1] = west_edge
    edges[2] = face_edge
    packs[0] = squeeze_rows(east_edge, lane)
    packs[1] = squeeze_rows(
        jnp.where(lane < TILES, west_edge, pltpu.roll(face_edge, TILES, 1)), lane
    )
    rows = chosen_rows(rows_ref)
    low = jnp.zeros((ROWS, WIDTH), F32)
    high = jnp.zeros((ROWS, WIDTH), F32)
    for p in range(POLE):
        picked = [edges[e, pl.ds(rows[p], 1), :] for e in range(3)]
        tile = jnp.where(row == 5, spread(picked[0]), jnp.where(row == 6, spread(picked[1]), spread(picked[2])))
        start = TILES * p
        moved = pltpu.roll(tile, start, 1) if start else tile
        low = jnp.where((lane >= start) & (lane < start + TILES), moved, low)
        if start + TILES > 100:
            moved = pltpu.roll(tile, (start - 100) % WIDTH, 1)
            high = jnp.where((lane >= start - 100) & (lane < start - 100 + TILES), moved, high)
    for j in range(RING):
        start = SHARE * j
        source, offset = (low, start) if start + SHARE <= WIDTH else (high, start - 100)
        moved = pltpu.roll(source, (WIDTH - offset) % WIDTH, 1) if offset else source
        sent[j, SHARE:, :] = moved[SHARE:]
        for i in range(SHARE):
            n = start + i
            if n < CIRCLES:
                sent[j, i : i + 1, :] = partial[n % TILES, pl.ds(rows[n // TILES], 1), :]
            else:
                sent[j, i : i + 1, :] = jnp.zeros((1, WIDTH), F32)


def filter_kernel(received, packs, inner, outer, weight_ref, returned, parts):
    me = lax.axis_index("lon")
    block = received[...]
    cosine, sine = inner[0], inner[1]
    flat = block.reshape(RING * ROWS, WIDTH)
    parts[...] = jnp.dot(
        flat,
        jnp.concatenate([cosine, sine], axis=1),
        precision=PRECISE,
        preferred_element_type=F32,
    )
    cosine_part = jnp.zeros((ROWS, MODES), F32)
    sine_part = jnp.zeros((ROWS, MODES), F32)
    for q in range(RING):
        c, s = outer[0, q : q + 1, :], outer[1, q : q + 1, :]
        own_c = parts[ROWS * q : ROWS * (q + 1), :MODES]
        own_s = parts[ROWS * q : ROWS * (q + 1), MODES:]
        cosine_part += c * own_c - s * own_s
        sine_part += s * own_c + c * own_s
    east_cells = received[:, 5, :]
    west_cells = received[:, 6, :]
    faces = received[:, 7, :]
    beyond = pltpu.roll(east_cells, 1, 0)
    flux = jnp.maximum(faces, 0.0) * beyond + jnp.minimum(faces, 0.0) * west_cells
    flux_lane = lax.broadcasted_iota(jnp.int32, flux.shape, 1)
    flux = jnp.where(flux_lane < SHARE, flux, 0.0)
    edge = lax.dot_general(
        flux,
        jnp.concatenate([outer[2], outer[3]], axis=1),
        (((0,), (0,)), ((), ())),
        precision=PRECISE,
        preferred_element_type=F32,
    )
    cosine_part += edge[:ROWS, :MODES]
    sine_part += edge[:ROWS, MODES:]
    weight = weight_ref[...]
    cosine_part *= weight
    sine_part *= weight
    for q in range(RING):
        c, s = outer[0, q : q + 1, :], outer[1, q : q + 1, :]
        parts[ROWS * q : ROWS * (q + 1), :MODES] = cosine_part * c + sine_part * s
        parts[ROWS * q : ROWS * (q + 1), MODES:] = sine_part * c - cosine_part * s
    smooth = jnp.dot(
        parts[...],
        jnp.concatenate([cosine, sine], axis=0),
        precision=PRECISE,
        preferred_element_type=F32,
    )
    returned[...] = smooth.reshape(RING, ROWS, WIDTH)
    returned[(me + 1) % RING, SHARE:, :] = packs[0, SHARE:, :]
    returned[(me + RING - 1) % RING, SHARE:, :] = packs[1, SHARE:, :]


def mend_kernel(burden, merid, halo_b, partial, mended):
    lane, row = iotas()
    even = lax.axis_index("lat") % 2 == 0
    edge = row == jnp.where(even, 0, ROWS - 1)
    for k in range(LEVELS):
        beyond = halo_b[TILES + k]
        face = jnp.where(even, merid[k], spread(beyond))
        up, down = jnp.maximum(face, 0.0), jnp.minimum(face, 0.0)
        for b in range(BINS):
            t = b * LEVELS + k
            cells = spread(halo_b[t])
            flux = jnp.where(even, up * cells, -(up * burden[t] + down * cells))
            mended[t] = partial[t] + jnp.where(edge, flux, 0.0)


def modes_kernel(pair, across, rising, falling, levels, rise, fall):
    me = lax.axis_index("lev")
    bottom = me < 2
    for k in range(2 * LEVELS):
        levels[k] = jnp.where(bottom, pair[k], across[k])
        levels[2 * LEVELS + k] = jnp.where(bottom, across[k], pair[k])
    depth = 4 * LEVELS
    inverse = [None] + [1.0 / levels[k] for k in range(1, depth)]
    up = jnp.ones((ROWS, WIDTH), F32)
    flux = up
    rise[0] = up
    for k in range(1, depth):
        up = up + flux * inverse[k]
        flux = flux + up
        rise[k] = up
    down = 1.0 / flux
    fall[depth - 1] = down
    flux = down
    for k in range(depth - 1, 0, -1):
        down = down + flux * inverse[k]
        flux = flux + down
        fall[k - 1] = down
    rising[...] = rise[pl.ds(LEVELS * me, LEVELS)]
    falling[...] = fall[pl.ds(LEVELS * me, LEVELS)]


def join_kernel(own, other, pair):
    lower = lax.axis_index("lev") % 2 == 0
    for k in range(LEVELS):
        pair[k] = jnp.where(lower, own[k], other[k])
        pair[LEVELS + k] = jnp.where(lower, other[k], own[k])


def column_kernel(mended, edges, back, code, rising, falling, local, outward):
    lane, row = iotas()
    me = lax.axis_index("lon")
    lev = lax.axis_index("lev")
    east_own, west_own, face_own = edges[0], edges[1], edges[2]
    from_west = unsqueeze_rows(back[(me + RING - 1) % RING], row)
    from_east = unsqueeze_rows(back[(me + 1) % RING], row)
    four = jnp.where(lane < LEVELS, pltpu.roll(from_east, WIDTH - TILES, 1), 0.0)
    eight = four + pltpu.roll(four, 4, 1)
    sixteen = eight + pltpu.roll(eight, 8, 1)
    face_next = sixteen + pltpu.roll(sixteen, 16, 1) + pltpu.roll(four, 32, 1)
    flux_in = jnp.maximum(face_own, 0.0) * from_west + jnp.minimum(face_own, 0.0) * west_own
    flux_out = jnp.maximum(face_next, 0.0) * east_own + jnp.minimum(face_next, 0.0) * from_east
    slot = code[...]
    here = [slot == p for p in range(POLE)]
    for b in range(BINS):
        source = []
        for k in range(LEVELS):
            t = b * LEVELS + k
            value = (
                mended[t]
                + jnp.where(lane == 0, column(flux_in, t), 0.0)
                - jnp.where(lane == WIDTH - 1, column(flux_out, t), 0.0)
            )
            for p in range(POLE):
                n = p * TILES + t
                smooth = back[n // SHARE, n % SHARE : n % SHARE + 1, :]
                value = jnp.where(here[p], spread(smooth), value)
            source.append(value)
        before = []
        total = jnp.zeros((ROWS, WIDTH), F32)
        for k in range(LEVELS):
            total = total + rising[k] * source[k]
            before.append(falling[k] * total)
        after = jnp.zeros((ROWS, WIDTH), F32)
        for k in range(LEVELS - 1, -1, -1):
            local[b * LEVELS + k] = before[k] + rising[k] * after
            after = after + falling[k] * source[k]
        for other in range(4):
            outward[other, b] = jnp.where(lev < other, total, after)


def phase_kernel(inward, local, rising, falling, threshold, inert, condensed, gas):
    lev = lax.axis_index("lev")
    from_below, from_above = [], []
    for b in range(BINS):
        below = jnp.zeros((ROWS, WIDTH), F32)
        above = jnp.zeros((ROWS, WIDTH), F32)
        for other in range(4):
            below = below + jnp.where(other < lev, inward[other, b], 0.0)
            above = above + jnp.where(other > lev, inward[other, b], 0.0)
        from_below.append(below)
        from_above.append(above)
    for k in range(LEVELS):
        up, down, emitted = rising[k], falling[k], inert[k]
        totals = [local[b * LEVELS + k] + down * from_below[b] + up * from_above[b] for b in range(BINS)]
        limit = [threshold[b * LEVELS + k] for b in range(BINS)]
        organic = emitted
        for _ in range(PITERS):
            held = totals[0] / (organic + limit[0])
            for b in range(1, BINS):
                held = held + totals[b] / (organic + limit[b])
            organic = emitted + organic * held
        for b in range(BINS):
            particle = totals[b] * (organic / (organic + limit[b]))
            condensed[b * LEVELS + k] = particle
            gas[b * LEVELS + k] = totals[b] - particle


def body(
    bin_burden,
    zonal_cfl_ratio,
    meridional_cfl_ratio,
    thermal_kelvins,
    diffusion_coefficient,
    inert_emitted_aerosol,
    heat_of_evaporation,
    damped_parallels,
    preserved_harmonic_limits,
):
    burden = bin_burden.reshape(TILES, ROWS, WIDTH)
    inner, outer = tables()
    field = shape(TILES, ROWS, WIDTH)
    tile = (ROWS, WIDTH)
    swap = [(0, 1), (1, 0), (2, 3), (3, 2)]
    cross = [(0, 3), (3, 0), (1, 2), (2, 1)]
    out_a, out_b = call(
        edge_kernel,
        "edge",
        (shape(GROUP, 1, WIDTH), shape(GROUP, 1, WIDTH)),
        [HBM] * 2,
        [pltpu.SemaphoreType.DMA((4,))],
    )(burden, meridional_cfl_ratio)
    halo_a = lax.ppermute(out_a, "lat", swap)
    weight, code, threshold = call(
        setup_kernel,
        "setup",
        (shape(*tile), jax.ShapeDtypeStruct(tile, jnp.int32), field),
        [SMEM] * 3 + [VMEM],
    )(damped_parallels, preserved_harmonic_limits, heat_of_evaporation, thermal_kelvins)
    partial, sent, edges, packs = call(
        advect_kernel,
        "advect",
        (field, shape(RING, *tile), shape(3, *tile), shape(2, *tile)),
        [SMEM] + [VMEM] * 4,
    )(damped_parallels, burden, zonal_cfl_ratio, meridional_cfl_ratio, halo_a)
    sent, out_b, mixing = lax.optimization_barrier((sent, out_b, diffusion_coefficient))
    received = lax.all_to_all(sent, "lon", 0, 0, tiled=True)
    halo_b = lax.ppermute(out_b, "lat", [(1, 2), (2, 1)])
    pair = call(join_kernel, "join", (shape(2 * LEVELS, *tile),), [VMEM] * 2)(
        mixing, lax.ppermute(mixing, "lev", swap)
    )[0]
    mended = call(mend_kernel, "mend", (field,), [VMEM] * 4)(
        burden, meridional_cfl_ratio, halo_b, partial
    )[0]
    returned = call(
        filter_kernel,
        "filter",
        (shape(RING, *tile),),
        [VMEM] * 5,
        [pltpu.VMEM((RING * ROWS, 2 * MODES), F32)],
    )(received, packs, inner, outer, weight)[0]
    returned, pair = lax.optimization_barrier((returned, pair))
    rising, falling = call(
        modes_kernel,
        "modes",
        (shape(LEVELS, *tile), shape(LEVELS, *tile)),
        [VMEM] * 2,
        [pltpu.VMEM((4 * LEVELS, *tile), F32)] * 3,
    )(pair, lax.ppermute(pair, "lev", cross))
    back = lax.all_to_all(returned, "lon", 0, 0, tiled=True)
    local, outward = call(
        column_kernel, "column", (field, shape(4, BINS, *tile)), [VMEM] * 6
    )(mended, edges, back, code, rising, falling)
    condensed, gas = call(phase_kernel, "phase", (field, field), [VMEM] * 6)(
        lax.all_to_all(outward, "lev", 0, 0, tiled=True),
        local,
        rising,
        falling,
        threshold,
        inert_emitted_aerosol,
    )
    return condensed.reshape(bin_burden.shape), gas.reshape(bin_burden.shape)


def solution(mesh):
    block = P("lev", "lat", "lon")
    binned = P(None, "lev", "lat", "lon")
    return jax.shard_map(
        body,
        mesh=mesh,
        in_specs=(binned, block, block, block, block, block, P(), P(), P()),
        out_specs=(binned, binned),
        check_vma=False,
    )
```

```python
import math

import jax
import jax.numpy as jnp
import numpy as np
from jax import lax
from jax.experimental import pallas as pl
from jax.experimental.pallas import tpu as pltpu
from jax.sharding import PartitionSpec as P

BINS = 9
LEVELS = 4
TILES = BINS * LEVELS
ROWS = 8
WIDTH = 128
RING = 32
POLE = 4
CIRCLES = POLE * TILES
SHARE = 5
MODES = 128
CIRCLE = RING * WIDTH
PITERS = 3
GAS_CONST = 0.008314
REF_TEMP = 298.0
PRECISE = lax.Precision.HIGHEST
F32 = jnp.float32
VMEM = pl.BlockSpec(memory_space=pltpu.VMEM)
GROUP = 40


def shape(*dims):
    return jax.ShapeDtypeStruct(dims, F32)


def call(kernel, name, outs, in_specs, scratch=(), flops=10**7):
    return pl.pallas_call(
        kernel,
        out_shape=outs,
        in_specs=in_specs,
        out_specs=tuple(VMEM for _ in outs),
        scratch_shapes=list(scratch),
        compiler_params=pltpu.CompilerParams(vmem_limit_bytes=16 * 2**20),
        cost_estimate=pl.CostEstimate(flops=flops, bytes_accessed=10**5, transcendentals=0),
        name=name,
    )


def tables():
    modes = np.arange(MODES)

    def pair(columns):
        angle = (columns[:, None] * modes[None, :] % CIRCLE) * (2.0 * math.pi / CIRCLE)
        return np.cos(angle), np.sin(angle)

    inner = np.stack(pair(np.arange(WIDTH))).astype(np.float32)
    first = pair(np.arange(RING) * WIDTH)
    before = pair(np.arange(RING) * WIDTH - 1)
    outer = np.stack([first[0], first[1], first[0] - before[0], first[1] - before[1]])
    return jnp.asarray(inner), jnp.asarray(outer.astype(np.float32))


def iotas():
    lane = lax.broadcasted_iota(jnp.int32, (ROWS, WIDTH), 1)
    row = lax.broadcasted_iota(jnp.int32, (ROWS, WIDTH), 0)
    return lane, row


def spread(row_vector):
    return jnp.broadcast_to(row_vector, (ROWS, WIDTH))


def column(tile, at):
    return jnp.broadcast_to(tile[:, at : at + 1], (ROWS, WIDTH))


def chosen_rows(settings):
    southern = lax.axis_index("lat") >= 2
    rows = settings[...]
    return [
        jnp.clip(
            jnp.where(southern, rows[0, POLE + p] - 3 * ROWS, rows[0, p]), 0, ROWS - 1
        )
        for p in range(POLE)
    ]


def blank_kernel(out):
    out[...] = jnp.zeros((ROWS, WIDTH), F32)


def edge_kernel(blank, rows, limits, burden, merid, out_a, out_b, settings):
    settings[0:1, : 2 * POLE] = rows[...]
    settings[1:2, : 2 * POLE] = limits[...]
    even = lax.axis_index("lat") % 2 == 0
    row_a = jnp.where(even, ROWS - 1, 0)
    row_b = ROWS - 1 - row_a
    for t in range(TILES):
        out_a[t] = burden[t, pl.ds(row_a, 1), :]
        out_b[t] = burden[t, pl.ds(row_b, 1), :]
    for k in range(LEVELS):
        out_a[TILES + k] = merid[k, pl.ds(row_a, 1), :]
        out_b[TILES + k] = merid[k, pl.ds(row_b, 1), :]


def threshold_kernel(heat, kelvins, threshold):
    for k in range(LEVELS):
        inverse = 1.0 / kelvins[k]
        ratio = REF_TEMP * inverse
        slope = (1.0 / REF_TEMP - inverse) * (1.0 / GAS_CONST)
        for b in range(BINS):
            rise = jnp.broadcast_to(heat[:, b : b + 1], (ROWS, WIDTH))
            threshold[b * LEVELS + k] = (10.0 ** (b - 2)) * ratio * jnp.exp(rise * slope)


def squeeze_rows(tile, lane):
    packed = jnp.zeros_like(tile)
    for g in range(3):
        moved = pltpu.roll(tile, (5 - 3 * g) % ROWS, 0)
        if g:
            moved = pltpu.roll(moved, GROUP * g, 1)
        packed = jnp.where((lane >= GROUP * g) & (lane < GROUP * (g + 1)), moved, packed)
    return packed


def unsqueeze_rows(packed, row):
    tile = jnp.zeros_like(packed)
    for g in range(3):
        moved = pltpu.roll(packed, (3 * g - 5) % ROWS, 0)
        if g:
            moved = pltpu.roll(moved, WIDTH - GROUP * g, 1)
        tile = jnp.where((row >= 3 * g) & (row < 3 * g + 3), moved, tile)
    return tile


def advect_kernel(settings, burden, zonal, merid, partial, edges, packs, faces, weight):
    lane, row = iotas()
    lat = lax.axis_index("lat")
    first_row = (row == 0) & (lat == 0)
    west_edge = jnp.zeros((ROWS, WIDTH), F32)
    east_edge = jnp.zeros((ROWS, WIDTH), F32)
    face_edge = jnp.zeros((ROWS, WIDTH), F32)
    for k in range(LEVELS):
        face = zonal[k]
        inner = jnp.where(lane == 0, 0.0, face)
        up, down = jnp.maximum(inner, 0.0), jnp.minimum(inner, 0.0)
        south = jnp.where(first_row, 0.0, merid[k])
        south_up = jnp.where(row == 0, 0.0, jnp.maximum(south, 0.0))
        south_down = jnp.minimum(south, 0.0)
        face_edge = jnp.where((lane < TILES) & (lane % LEVELS == k), column(face, 0), face_edge)
        for b in range(BINS):
            t = b * LEVELS + k
            tile = burden[t]
            west = up * pltpu.roll(tile, 1, 1) + down * tile
            from_south = south_up * pltpu.roll(tile, 1, 0) + south_down * tile
            to_north = jnp.where(row == ROWS - 1, 0.0, pltpu.roll(from_south, ROWS - 1, 0))
            partial[t] = (
                tile + west - pltpu.roll(west, WIDTH - 1, 1) + from_south - to_north
            )
            west_edge = jnp.where(lane == t, column(tile, 0), west_edge)
            east_edge = jnp.where(lane == t, column(tile, WIDTH - 1), east_edge)
    edges[0] = east_edge
    edges[1] = west_edge
    edges[2] = face_edge
    packs[0] = squeeze_rows(east_edge, lane)
    packs[1] = squeeze_rows(
        jnp.where(lane < TILES, west_edge, pltpu.roll(face_edge, TILES, 1)), lane
    )
    me = lax.axis_index("lon")
    southern = lat >= 2
    number = SHARE * me + row
    limit = jnp.zeros((ROWS, MODES), jnp.int32)
    for p in range(POLE):
        kept = jnp.where(southern, settings[1:2, POLE + p : POLE + p + 1], settings[1:2, p : p + 1])
        limit = jnp.where(number >= p * TILES, jnp.broadcast_to(kept, (ROWS, MODES)), limit)
    weight[...] = jnp.where(lane < limit, jnp.where(lane == 0, 1.0, 2.0), 0.0) * (1.0 / CIRCLE)
    rows = chosen_rows(settings)
    low = jnp.zeros((ROWS, WIDTH), F32)
    high = jnp.zeros((ROWS, WIDTH), F32)
    for p in range(POLE):
        picked = [edges[e, pl.ds(rows[p], 1), :] for e in range(3)]
        tile = jnp.where(row == 5, spread(picked[0]), jnp.where(row == 6, spread(picked[1]), spread(picked[2])))
        start = TILES * p
        moved = pltpu.roll(tile, start, 1) if start else tile
        low = jnp.where((lane >= start) & (lane < start + TILES), moved, low)
        if start + TILES > 100:
            moved = pltpu.roll(tile, (start - 100) % WIDTH, 1)
            high = jnp.where((lane >= start - 100) & (lane < start - 100 + TILES), moved, high)
    for j in range(RING):
        start = SHARE * j
        source, offset = (low, start) if start + SHARE <= WIDTH else (high, start - 100)
        faces[j] = pltpu.roll(source, (WIDTH - offset) % WIDTH, 1) if offset else source


def border(t, k, at_south, row, halo, burden, merid):
    beyond = spread(halo[TILES + k])
    cells = spread(halo[t])
    face = jnp.where(at_south, merid[k], beyond)
    up, down = jnp.maximum(face, 0.0), jnp.minimum(face, 0.0)
    flux = jnp.where(at_south, up * cells, -(up * burden[t] + down * cells))
    return jnp.where(row == jnp.where(at_south, 0, ROWS - 1), flux, 0.0)


def pack_kernel(settings, burden, merid, halo_a, halo_b, partial, faces, bordered, sent):
    lane, row = iotas()
    odd = lax.axis_index("lat") % 2 == 1
    for t in range(TILES):
        k = t % LEVELS
        bordered[t] = (
            partial[t]
            + border(t, k, odd, row, halo_a, burden, merid)
            + border(t, k, ~odd, row, halo_b, burden, merid)
        )
    rows = chosen_rows(settings)
    for j in range(RING):
        sent[j, SHARE:, :] = faces[j, SHARE:, :]
        for i in range(SHARE):
            n = SHARE * j + i
            if n < CIRCLES:
                sent[j, i : i + 1, :] = bordered[n % TILES, pl.ds(rows[n // TILES], 1), :]
            else:
                sent[j, i : i + 1, :] = jnp.zeros((1, WIDTH), F32)


def filter_kernel(received, packs, inner, outer, weight_ref, returned, parts):
    me = lax.axis_index("lon")
    block = received[...]
    cosine, sine = inner[0], inner[1]
    flat = block.reshape(RING * ROWS, WIDTH)
    parts[...] = jnp.dot(
        flat,
        jnp.concatenate([cosine, sine], axis=1),
        precision=PRECISE,
        preferred_element_type=F32,
    )
    cosine_part = jnp.zeros((ROWS, MODES), F32)
    sine_part = jnp.zeros((ROWS, MODES), F32)
    for q in range(RING):
        c, s = outer[0, q : q + 1, :], outer[1, q : q + 1, :]
        own_c = parts[ROWS * q : ROWS * (q + 1), :MODES]
        own_s = parts[ROWS * q : ROWS * (q + 1), MODES:]
        cosine_part += c * own_c - s * own_s
        sine_part += s * own_c + c * own_s
    east_cells = received[:, 5, :]
    west_cells = received[:, 6, :]
    faces = received[:, 7, :]
    beyond = pltpu.roll(east_cells, 1, 0)
    flux = jnp.maximum(faces, 0.0) * beyond + jnp.minimum(faces, 0.0) * west_cells
    flux_lane = lax.broadcasted_iota(jnp.int32, flux.shape, 1)
    flux = jnp.where(flux_lane < SHARE, flux, 0.0)
    edge = lax.dot_general(
        flux,
        jnp.concatenate([outer[2], outer[3]], axis=1),
        (((0,), (0,)), ((), ())),
        precision=PRECISE,
        preferred_element_type=F32,
    )
    cosine_part += edge[:ROWS, :MODES]
    sine_part += edge[:ROWS, MODES:]
    weight = weight_ref[...]
    cosine_part *= weight
    sine_part *= weight
    for q in range(RING):
        c, s = outer[0, q : q + 1, :], outer[1, q : q + 1, :]
        parts[ROWS * q : ROWS * (q + 1), :MODES] = cosine_part * c + sine_part * s
        parts[ROWS * q : ROWS * (q + 1), MODES:] = sine_part * c - cosine_part * s
    smooth = jnp.dot(
        parts[...],
        jnp.concatenate([cosine, sine], axis=0),
        precision=PRECISE,
        preferred_element_type=F32,
    )
    returned[...] = smooth.reshape(RING, ROWS, WIDTH)
    returned[(me + 1) % RING, SHARE:, :] = packs[0, SHARE:, :]
    returned[(me + RING - 1) % RING, SHARE:, :] = packs[1, SHARE:, :]


def column_kernel(settings, bordered, edges, back, diffusion, local, response, payload):
    lane, row = iotas()
    me = lax.axis_index("lon")
    east_own, west_own, face_own = edges[0], edges[1], edges[2]
    from_west = unsqueeze_rows(back[(me + RING - 1) % RING], row)
    from_east = unsqueeze_rows(back[(me + 1) % RING], row)
    four = jnp.where(lane < LEVELS, pltpu.roll(from_east, WIDTH - TILES, 1), 0.0)
    eight = four + pltpu.roll(four, 4, 1)
    sixteen = eight + pltpu.roll(eight, 8, 1)
    face_next = sixteen + pltpu.roll(sixteen, 16, 1) + pltpu.roll(four, 32, 1)
    flux_in = jnp.maximum(face_own, 0.0) * from_west + jnp.minimum(face_own, 0.0) * west_own
    flux_out = jnp.maximum(face_next, 0.0) * east_own + jnp.minimum(face_next, 0.0) * from_east
    lat = lax.axis_index("lat")
    active = (lat == 0) | (lat == 3)
    here = []
    for p in range(POLE):
        north, south = settings[0:1, p : p + 1], settings[0:1, POLE + p : POLE + p + 1] - 3 * ROWS
        chosen = jnp.broadcast_to(jnp.where(lat == 0, north, south), (ROWS, WIDTH))
        here.append((row == chosen) & active)
    a1, a2, a3 = diffusion[1], diffusion[2], diffusion[3]
    i0 = 1.0 / (1.0 + a1)
    w1 = a1 * i0
    e1 = 1.0 + w1
    i1 = 1.0 / (e1 + a2)
    w2 = a2 * i1
    e2 = 1.0 + w2 * e1
    i2 = 1.0 / (e2 + a3)
    w3 = a3 * i2
    i3 = 1.0 / (1.0 + w3 * e2)
    up3 = i3
    up2 = w3 * up3
    up1 = w2 * up2
    up0 = w1 * up1
    d2 = w2 * w1
    low3 = w3 * d2 * i3
    low2 = d2 * i2 + w3 * low3
    low1 = w1 * i1 + w2 * low2
    low0 = i0 + w1 * low1
    for at, value in enumerate((low0, low1, low2, low3, up0, up1, up2, up3)):
        response[at] = value
    for b in range(BINS):
        source = []
        for k in range(LEVELS):
            t = b * LEVELS + k
            value = (
                bordered[t]
                + jnp.where(lane == 0, column(flux_in, t), 0.0)
                - jnp.where(lane == WIDTH - 1, column(flux_out, t), 0.0)
            )
            for p in range(POLE):
                n = p * TILES + t
                smooth = back[n // SHARE, n % SHARE : n % SHARE + 1, :]
                value = jnp.where(here[p], spread(smooth), value)
            source.append(value)
        f0 = source[0]
        f1 = source[1] + w1 * f0
        f2 = source[2] + w2 * f1
        f3 = source[3] + w3 * f2
        x3 = f3 * i3
        x2 = f2 * i2 + w3 * x3
        x1 = f1 * i1 + w2 * x2
        x0 = f0 * i0 + w1 * x1
        local[b * LEVELS] = x0
        local[b * LEVELS + 1] = x1
        local[b * LEVELS + 2] = x2
        local[b * LEVELS + 3] = x3
        payload[b] = x0
        payload[BINS + b] = x3
    payload[2 * BINS] = low0
    payload[2 * BINS + 1] = up3
    payload[2 * BINS + 2] = up0
    payload[2 * BINS + 3] = 1.0 / diffusion[0]


def pair_kernel(own, other, payload, inside):
    lev = lax.axis_index("lev")
    lower = lev % 2 == 0
    bottom = lev < 2

    def of_lower(at):
        return jnp.where(lower, own[at], other[at])

    def of_upper(at):
        return jnp.where(lower, other[at], own[at])

    scale = 1.0 / (of_upper(2 * BINS + 3) + of_lower(2 * BINS + 1) + of_upper(2 * BINS))
    through = jnp.where(bottom, of_upper(2 * BINS + 2), of_lower(2 * BINS + 2))
    coupling = through * scale
    facing = jnp.where(bottom, of_upper(2 * BINS + 1), of_lower(2 * BINS))
    sign = jnp.where(bottom, 1.0, -1.0)
    signed = through * sign
    inside[BINS] = coupling
    payload[BINS] = facing - through * coupling
    payload[BINS + 1] = jnp.where(bottom, 0.0, of_lower(2 * BINS + 3))
    for b in range(BINS):
        flux = (of_lower(BINS + b) - of_upper(b)) * scale
        inside[b] = flux
        payload[b] = jnp.where(bottom, of_upper(BINS + b), of_lower(b)) + signed * flux


def phase_kernel(own, other, inside, local, response, threshold, inert, condensed, gas):
    lev = lax.axis_index("lev")
    lower = lev % 2 == 0
    middle = (lev == 1) | (lev == 2)
    sign = jnp.where(lev < 2, 1.0, -1.0)
    scale = sign / (own[BINS + 1] + other[BINS + 1] + own[BINS] + other[BINS])
    below, above = [], []
    for b in range(BINS):
        centre = (own[b] - other[b]) * scale
        mid = inside[b] + inside[BINS] * centre
        open_end = jnp.where(middle, centre, 0.0)
        below.append(jnp.where(lower, open_end, mid))
        above.append(jnp.where(lower, mid, open_end))
    for k in range(LEVELS):
        low, up, emitted = response[k], response[LEVELS + k], inert[k]
        totals = [local[b * LEVELS + k] + low * below[b] - up * above[b] for b in range(BINS)]
        limit = [threshold[b * LEVELS + k] for b in range(BINS)]
        organic = emitted
        for _ in range(PITERS):
            held = totals[0] / (organic + limit[0])
            for b in range(1, BINS):
                held = held + totals[b] / (organic + limit[b])
            organic = emitted + organic * held
        for b in range(BINS):
            particle = totals[b] * (organic / (organic + limit[b]))
            condensed[b * LEVELS + k] = particle
            gas[b * LEVELS + k] = totals[b] - particle


def body(
    bin_burden,
    zonal_cfl_ratio,
    meridional_cfl_ratio,
    thermal_kelvins,
    diffusion_coefficient,
    inert_emitted_aerosol,
    heat_of_evaporation,
    damped_parallels,
    preserved_harmonic_limits,
):
    burden = bin_burden.reshape(TILES, ROWS, WIDTH)
    inner, outer = tables()
    field = shape(TILES, ROWS, WIDTH)
    tile = (ROWS, WIDTH)
    swap = [(0, 1), (1, 0), (2, 3), (3, 2)]
    cross = [(0, 3), (3, 0), (1, 2), (2, 1)]
    out_a, out_b, settings = call(
        edge_kernel,
        "edge",
        (shape(GROUP, 1, WIDTH), shape(GROUP, 1, WIDTH), jax.ShapeDtypeStruct(tile, jnp.int32)),
        [VMEM] * 5,
    )(
        call(blank_kernel, "blank", (shape(*tile),), [], flops=4 * 10**9)()[0],
        damped_parallels.reshape(1, 2 * POLE),
        preserved_harmonic_limits.reshape(1, 2 * POLE),
        burden,
        meridional_cfl_ratio,
    )
    halo_a = lax.ppermute(out_a, "lat", swap)
    halo_b = lax.ppermute(out_b, "lat", [(1, 2), (2, 1)])
    partial, edges, packs, faces, weight = call(
        advect_kernel,
        "advect",
        (field, shape(3, *tile), shape(2, *tile), shape(RING, *tile), shape(*tile)),
        [VMEM] * 4,
    )(settings, burden, zonal_cfl_ratio, meridional_cfl_ratio)
    halo_a, partial, faces = lax.optimization_barrier((halo_a, partial, faces))
    bordered, sent = call(
        pack_kernel, "pack", (field, shape(RING, *tile)), [VMEM] * 7
    )(settings, burden, meridional_cfl_ratio, halo_a, halo_b, partial, faces)
    received = lax.all_to_all(sent, "lon", 0, 0, tiled=True)
    returned = call(
        filter_kernel,
        "filter",
        (shape(RING, *tile),),
        [VMEM] * 5,
        [pltpu.VMEM((RING * ROWS, 2 * MODES), F32)],
    )(received, packs, inner, outer, weight)[0]
    back = lax.all_to_all(returned, "lon", 0, 0, tiled=True)
    count = 2 * BINS + 4
    local, response, payload = call(
        column_kernel,
        "column",
        (field, shape(2 * LEVELS, *tile), shape(count, *tile)),
        [VMEM] * 5,
    )(settings, bordered, edges, back, diffusion_coefficient)
    payload, kelvins = lax.optimization_barrier((payload, thermal_kelvins))
    partner = lax.ppermute(payload, "lev", swap)
    threshold = call(threshold_kernel, "threshold", (field,), [VMEM] * 2)(
        heat_of_evaporation.reshape(1, BINS), kelvins
    )[0]
    partner, threshold = lax.optimization_barrier((partner, threshold))
    facing, inside = call(
        pair_kernel,
        "pair",
        (shape(BINS + 2, *tile), shape(BINS + 1, *tile)),
        [VMEM] * 2,
    )(payload, partner)
    condensed, gas = call(phase_kernel, "phase", (field, field), [VMEM] * 7)(
        facing,
        lax.ppermute(facing, "lev", cross),
        inside,
        local,
        response,
        threshold,
        inert_emitted_aerosol,
    )
    return condensed.reshape(bin_burden.shape), gas.reshape(bin_burden.shape)


def solution(mesh):
    block = P("lev", "lat", "lon")
    binned = P(None, "lev", "lat", "lon")
    return jax.shard_map(
        body,
        mesh=mesh,
        in_specs=(binned, block, block, block, block, block, P(), P(), P()),
        out_specs=(binned, binned),
        check_vma=False,
    )
```

```python
import math

import jax
import jax.numpy as jnp
import numpy as np
from jax import lax
from jax.experimental import pallas as pl
from jax.experimental.pallas import tpu as pltpu
from jax.sharding import PartitionSpec as P

BINS = 9
LEVELS = 4
TILES = BINS * LEVELS
ROWS = 8
WIDTH = 128
RING = 32
POLE = 4
CIRCLES = POLE * TILES
SHARE = 5
MODES = 128
CIRCLE = RING * WIDTH
PITERS = 3
GAS_CONST = 0.008314
REF_TEMP = 298.0
PRECISE = lax.Precision.HIGHEST
F32 = jnp.float32
VMEM = pl.BlockSpec(memory_space=pltpu.VMEM)
GROUP = 40


def shape(*dims):
    return jax.ShapeDtypeStruct(dims, F32)


def call(kernel, name, outs, in_specs, scratch=(), flops=10**7, place=VMEM):
    return pl.pallas_call(
        kernel,
        out_shape=outs,
        in_specs=in_specs,
        out_specs=tuple(place for _ in outs),
        scratch_shapes=list(scratch),
        compiler_params=pltpu.CompilerParams(vmem_limit_bytes=16 * 2**20),
        cost_estimate=pl.CostEstimate(flops=flops, bytes_accessed=10**5, transcendentals=0),
        name=name,
    )


def tables():
    modes = np.arange(MODES)

    def pair(columns):
        angle = (columns[:, None] * modes[None, :] % CIRCLE) * (2.0 * math.pi / CIRCLE)
        return np.cos(angle), np.sin(angle)

    inner = np.stack(pair(np.arange(WIDTH))).astype(np.float32)
    first = pair(np.arange(RING) * WIDTH)
    before = pair(np.arange(RING) * WIDTH - 1)
    outer = np.stack([first[0], first[1], first[0] - before[0], first[1] - before[1]])
    return jnp.asarray(inner), jnp.asarray(outer.astype(np.float32))


def iotas():
    lane = lax.broadcasted_iota(jnp.int32, (ROWS, WIDTH), 1)
    row = lax.broadcasted_iota(jnp.int32, (ROWS, WIDTH), 0)
    return lane, row


def spread(row_vector):
    return jnp.broadcast_to(row_vector, (ROWS, WIDTH))


def column(tile, at):
    return jnp.broadcast_to(tile[:, at : at + 1], (ROWS, WIDTH))


def chosen_rows(settings):
    southern = lax.axis_index("lat") >= 2
    rows = settings[...]
    return [
        jnp.clip(
            jnp.where(southern, rows[0, POLE + p] - 3 * ROWS, rows[0, p]), 0, ROWS - 1
        )
        for p in range(POLE)
    ]


def blank_kernel(out):
    out[...] = jnp.zeros((ROWS, WIDTH), F32)


def edge_kernel(blank, rows, limits, burden, merid, out_a, out_b, settings):
    settings[0:1, : 2 * POLE] = rows[...]
    settings[1:2, : 2 * POLE] = limits[...]
    even = lax.axis_index("lat") % 2 == 0
    row_a = jnp.where(even, ROWS - 1, 0)
    row_b = ROWS - 1 - row_a
    for t in range(TILES):
        out_a[t] = burden[t, pl.ds(row_a, 1), :]
        out_b[t] = burden[t, pl.ds(row_b, 1), :]
    for k in range(LEVELS):
        out_a[TILES + k] = merid[k, pl.ds(row_a, 1), :]
        out_b[TILES + k] = merid[k, pl.ds(row_b, 1), :]


def threshold_kernel(heat, kelvins, threshold):
    for k in range(LEVELS):
        inverse = 1.0 / kelvins[k]
        ratio = REF_TEMP * inverse
        slope = (1.0 / REF_TEMP - inverse) * (1.0 / GAS_CONST)
        for b in range(BINS):
            rise = jnp.broadcast_to(heat[:, b : b + 1], (ROWS, WIDTH))
            threshold[b * LEVELS + k] = (10.0 ** (b - 2)) * ratio * jnp.exp(rise * slope)


def squeeze_rows(tile, lane):
    packed = jnp.zeros_like(tile)
    for g in range(3):
        moved = pltpu.roll(tile, (5 - 3 * g) % ROWS, 0)
        if g:
            moved = pltpu.roll(moved, GROUP * g, 1)
        packed = jnp.where((lane >= GROUP * g) & (lane < GROUP * (g + 1)), moved, packed)
    return packed


def unsqueeze_rows(packed, row):
    tile = jnp.zeros_like(packed)
    for g in range(3):
        moved = pltpu.roll(packed, (3 * g - 5) % ROWS, 0)
        if g:
            moved = pltpu.roll(moved, WIDTH - GROUP * g, 1)
        tile = jnp.where((row >= 3 * g) & (row < 3 * g + 3), moved, tile)
    return tile


def advect_kernel(settings, burden, zonal, merid, partial, edges, packs, faces, weight):
    lane, row = iotas()
    lat = lax.axis_index("lat")
    first_row = (row == 0) & (lat == 0)
    west_edge = jnp.zeros((ROWS, WIDTH), F32)
    east_edge = jnp.zeros((ROWS, WIDTH), F32)
    face_edge = jnp.zeros((ROWS, WIDTH), F32)
    for k in range(LEVELS):
        face = zonal[k]
        inner = jnp.where(lane == 0, 0.0, face)
        up, down = jnp.maximum(inner, 0.0), jnp.minimum(inner, 0.0)
        south = jnp.where(first_row, 0.0, merid[k])
        south_up = jnp.where(row == 0, 0.0, jnp.maximum(south, 0.0))
        south_down = jnp.minimum(south, 0.0)
        face_edge = jnp.where((lane < TILES) & (lane % LEVELS == k), column(face, 0), face_edge)
        for b in range(BINS):
            t = b * LEVELS + k
            tile = burden[t]
            west = up * pltpu.roll(tile, 1, 1) + down * tile
            from_south = south_up * pltpu.roll(tile, 1, 0) + south_down * tile
            to_north = jnp.where(row == ROWS - 1, 0.0, pltpu.roll(from_south, ROWS - 1, 0))
            partial[t] = (
                tile + west - pltpu.roll(west, WIDTH - 1, 1) + from_south - to_north
            )
            west_edge = jnp.where(lane == t, column(tile, 0), west_edge)
            east_edge = jnp.where(lane == t, column(tile, WIDTH - 1), east_edge)
    edges[0] = east_edge
    edges[1] = west_edge
    edges[2] = face_edge
    packs[0] = squeeze_rows(east_edge, lane)
    packs[1] = squeeze_rows(
        jnp.where(lane < TILES, west_edge, pltpu.roll(face_edge, TILES, 1)), lane
    )
    me = lax.axis_index("lon")
    southern = lat >= 2
    number = SHARE * me + row
    limit = jnp.zeros((ROWS, MODES), jnp.int32)
    for p in range(POLE):
        kept = jnp.where(southern, settings[1:2, POLE + p : POLE + p + 1], settings[1:2, p : p + 1])
        limit = jnp.where(number >= p * TILES, jnp.broadcast_to(kept, (ROWS, MODES)), limit)
    weight[...] = jnp.where(lane < limit, jnp.where(lane == 0, 1.0, 2.0), 0.0) * (1.0 / CIRCLE)
    rows = chosen_rows(settings)
    low = jnp.zeros((ROWS, WIDTH), F32)
    high = jnp.zeros((ROWS, WIDTH), F32)
    for p in range(POLE):
        picked = [edges[e, pl.ds(rows[p], 1), :] for e in range(3)]
        tile = jnp.where(row == 5, spread(picked[0]), jnp.where(row == 6, spread(picked[1]), spread(picked[2])))
        start = TILES * p
        moved = pltpu.roll(tile, start, 1) if start else tile
        low = jnp.where((lane >= start) & (lane < start + TILES), moved, low)
        if start + TILES > 100:
            moved = pltpu.roll(tile, (start - 100) % WIDTH, 1)
            high = jnp.where((lane >= start - 100) & (lane < start - 100 + TILES), moved, high)
    for j in range(RING):
        start = SHARE * j
        source, offset = (low, start) if start + SHARE <= WIDTH else (high, start - 100)
        faces[j] = pltpu.roll(source, (WIDTH - offset) % WIDTH, 1) if offset else source


def border(t, k, at_south, row, halo, burden, merid):
    beyond = spread(halo[TILES + k])
    cells = spread(halo[t])
    face = jnp.where(at_south, merid[k], beyond)
    up, down = jnp.maximum(face, 0.0), jnp.minimum(face, 0.0)
    flux = jnp.where(at_south, up * cells, -(up * burden[t] + down * cells))
    return jnp.where(row == jnp.where(at_south, 0, ROWS - 1), flux, 0.0)


def pack_kernel(settings, burden, merid, halo_a, partial, faces, inner, outer, bordered, sent):
    lane, row = iotas()
    odd = lax.axis_index("lat") % 2 == 1
    for t in range(TILES):
        k = t % LEVELS
        bordered[t] = partial[t] + border(t, k, odd, row, halo_a, burden, merid)
    rows = chosen_rows(settings)
    for j in range(RING):
        sent[j, SHARE:, :] = faces[j, SHARE:, :]
        for i in range(SHARE):
            n = SHARE * j + i
            if n < CIRCLES:
                sent[j, i : i + 1, :] = bordered[n % TILES, pl.ds(rows[n // TILES], 1), :]
            else:
                sent[j, i : i + 1, :] = jnp.zeros((1, WIDTH), F32)


def halves(values):
    high = values.astype(jnp.bfloat16)
    return high, (values - high.astype(F32)).astype(jnp.bfloat16)


def product(left, right):
    left_high, left_low = halves(left)
    right_high, right_low = halves(right)

    def dot(a, b):
        return jnp.dot(a, b, preferred_element_type=F32)

    return dot(left_high, right_high) + (dot(left_high, right_low) + dot(left_low, right_high))


def filter_kernel(received, packs, inner, outer, weight_ref, returned, parts):
    me = lax.axis_index("lon")
    lat = lax.axis_index("lat")
    active = (lat == 0) | (lat == 3)

    @pl.when(active)
    def _():
        block = received[...]
        cosine, sine = inner[0], inner[1]
        flat = block.reshape(RING * ROWS, WIDTH)
        parts[...] = product(flat, jnp.concatenate([cosine, sine], axis=1))
        cosine_part = jnp.zeros((ROWS, MODES), F32)
        sine_part = jnp.zeros((ROWS, MODES), F32)
        for q in range(RING):
            c, s = outer[0, q : q + 1, :], outer[1, q : q + 1, :]
            own_c = parts[ROWS * q : ROWS * (q + 1), :MODES]
            own_s = parts[ROWS * q : ROWS * (q + 1), MODES:]
            cosine_part += c * own_c - s * own_s
            sine_part += s * own_c + c * own_s
        east_cells = received[:, 5, :]
        west_cells = received[:, 6, :]
        faces = received[:, 7, :]
        beyond = pltpu.roll(east_cells, 1, 0)
        flux = jnp.maximum(faces, 0.0) * beyond + jnp.minimum(faces, 0.0) * west_cells
        flux_lane = lax.broadcasted_iota(jnp.int32, flux.shape, 1)
        flux = jnp.where(flux_lane < SHARE, flux, 0.0)
        edge = lax.dot_general(
            flux,
            jnp.concatenate([outer[2], outer[3]], axis=1),
            (((0,), (0,)), ((), ())),
            precision=PRECISE,
            preferred_element_type=F32,
        )
        cosine_part += edge[:ROWS, :MODES]
        sine_part += edge[:ROWS, MODES:]
        weight = weight_ref[...]
        cosine_part *= weight
        sine_part *= weight
        for q in range(RING):
            c, s = outer[0, q : q + 1, :], outer[1, q : q + 1, :]
            parts[ROWS * q : ROWS * (q + 1), :MODES] = cosine_part * c + sine_part * s
            parts[ROWS * q : ROWS * (q + 1), MODES:] = sine_part * c - cosine_part * s
        smooth = product(parts[...], jnp.concatenate([cosine, sine], axis=0))
        returned[...] = smooth.reshape(RING, ROWS, WIDTH)

    @pl.when(jnp.logical_not(active))
    def _():
        returned[...] = jnp.zeros((RING, ROWS, WIDTH), F32)

    returned[(me + 1) % RING, SHARE:, :] = packs[0, SHARE:, :]
    returned[(me + RING - 1) % RING, SHARE:, :] = packs[1, SHARE:, :]


def mend_kernel(burden, merid, halo_b, bordered, mended):
    lane, row = iotas()
    even = lax.axis_index("lat") % 2 == 0
    for t in range(TILES):
        mended[t] = bordered[t] + border(t, t % LEVELS, even, row, halo_b, burden, merid)


def column_kernel(settings, bordered, edges, back, diffusion, local, response, payload):
    lane, row = iotas()
    me = lax.axis_index("lon")
    east_own, west_own, face_own = edges[0], edges[1], edges[2]
    from_west = unsqueeze_rows(back[(me + RING - 1) % RING], row)
    from_east = unsqueeze_rows(back[(me + 1) % RING], row)
    four = jnp.where(lane < LEVELS, pltpu.roll(from_east, WIDTH - TILES, 1), 0.0)
    eight = four + pltpu.roll(four, 4, 1)
    sixteen = eight + pltpu.roll(eight, 8, 1)
    face_next = sixteen + pltpu.roll(sixteen, 16, 1) + pltpu.roll(four, 32, 1)
    flux_in = jnp.maximum(face_own, 0.0) * from_west + jnp.minimum(face_own, 0.0) * west_own
    flux_out = jnp.maximum(face_next, 0.0) * east_own + jnp.minimum(face_next, 0.0) * from_east
    lat = lax.axis_index("lat")
    active = (lat == 0) | (lat == 3)
    here = []
    for p in range(POLE):
        north, south = settings[0:1, p : p + 1], settings[0:1, POLE + p : POLE + p + 1] - 3 * ROWS
        chosen = jnp.broadcast_to(jnp.where(lat == 0, north, south), (ROWS, WIDTH))
        here.append((row == chosen) & active)
    a1, a2, a3 = diffusion[1], diffusion[2], diffusion[3]
    i0 = 1.0 / (1.0 + a1)
    w1 = a1 * i0
    e1 = 1.0 + w1
    i1 = 1.0 / (e1 + a2)
    w2 = a2 * i1
    e2 = 1.0 + w2 * e1
    i2 = 1.0 / (e2 + a3)
    w3 = a3 * i2
    i3 = 1.0 / (1.0 + w3 * e2)
    up3 = i3
    up2 = w3 * up3
    up1 = w2 * up2
    up0 = w1 * up1
    d2 = w2 * w1
    low3 = w3 * d2 * i3
    low2 = d2 * i2 + w3 * low3
    low1 = w1 * i1 + w2 * low2
    low0 = i0 + w1 * low1
    for at, value in enumerate((low0, low1, low2, low3, up0, up1, up2, up3)):
        response[at] = value
    for b in range(BINS):
        source = []
        for k in range(LEVELS):
            t = b * LEVELS + k
            value = (
                bordered[t]
                + jnp.where(lane == 0, column(flux_in, t), 0.0)
                - jnp.where(lane == WIDTH - 1, column(flux_out, t), 0.0)
            )
            for p in range(POLE):
                n = p * TILES + t
                smooth = back[n // SHARE, n % SHARE : n % SHARE + 1, :]
                value = jnp.where(here[p], spread(smooth), value)
            source.append(value)
        f0 = source[0]
        f1 = source[1] + w1 * f0
        f2 = source[2] + w2 * f1
        f3 = source[3] + w3 * f2
        x3 = f3 * i3
        x2 = f2 * i2 + w3 * x3
        x1 = f1 * i1 + w2 * x2
        x0 = f0 * i0 + w1 * x1
        local[b * LEVELS] = x0
        local[b * LEVELS + 1] = x1
        local[b * LEVELS + 2] = x2
        local[b * LEVELS + 3] = x3
        payload[b] = x0
        payload[BINS + b] = x3
    payload[2 * BINS] = low0
    payload[2 * BINS + 1] = up3
    payload[2 * BINS + 2] = up0
    payload[2 * BINS + 3] = 1.0 / diffusion[0]


def pair_kernel(own, other, payload, inside):
    lev = lax.axis_index("lev")
    lower = lev % 2 == 0
    bottom = lev < 2

    def of_lower(at):
        return jnp.where(lower, own[at], other[at])

    def of_upper(at):
        return jnp.where(lower, other[at], own[at])

    scale = 1.0 / (of_upper(2 * BINS + 3) + of_lower(2 * BINS + 1) + of_upper(2 * BINS))
    through = jnp.where(bottom, of_upper(2 * BINS + 2), of_lower(2 * BINS + 2))
    coupling = through * scale
    facing = jnp.where(bottom, of_upper(2 * BINS + 1), of_lower(2 * BINS))
    sign = jnp.where(bottom, 1.0, -1.0)
    signed = through * sign
    inside[BINS] = coupling
    payload[BINS] = facing - through * coupling
    payload[BINS + 1] = jnp.where(bottom, 0.0, of_lower(2 * BINS + 3))
    for b in range(BINS):
        flux = (of_lower(BINS + b) - of_upper(b)) * scale
        inside[b] = flux
        payload[b] = jnp.where(bottom, of_upper(BINS + b), of_lower(b)) + signed * flux


def phase_kernel(
    own, other, inside, local, response, threshold, inert, condensed, gas, particles, vapour, sems
):
    lev = lax.axis_index("lev")
    lower = lev % 2 == 0
    middle = (lev == 1) | (lev == 2)
    sign = jnp.where(lev < 2, 1.0, -1.0)
    scale = sign / (own[BINS + 1] + other[BINS + 1] + own[BINS] + other[BINS])
    below, above = [], []
    for b in range(BINS):
        centre = (own[b] - other[b]) * scale
        mid = inside[b] + inside[BINS] * centre
        open_end = jnp.where(middle, centre, 0.0)
        below.append(jnp.where(lower, open_end, mid))
        above.append(jnp.where(lower, mid, open_end))
    copies = []
    for k in range(LEVELS):
        low, up, emitted = response[k], response[LEVELS + k], inert[k]
        totals = [local[b * LEVELS + k] + low * below[b] - up * above[b] for b in range(BINS)]
        limit = [threshold[b * LEVELS + k] for b in range(BINS)]
        organic = emitted
        for _ in range(PITERS):
            held = totals[0] / (organic + limit[0])
            for b in range(1, BINS):
                held = held + totals[b] / (organic + limit[b])
            organic = emitted + organic * held
        for b in range(BINS):
            particle = totals[b] * (organic / (organic + limit[b]))
            particles[b, k] = particle
            vapour[b, k] = totals[b] - particle
        for at, (source, target) in enumerate(((particles, condensed), (vapour, gas))):
            copy = pltpu.make_async_copy(source.at[:, k], target.at[:, k], sems.at[k, at])
            copy.start()
            copies.append(copy)
    for copy in copies:
        copy.wait()


def body(
    bin_burden,
    zonal_cfl_ratio,
    meridional_cfl_ratio,
    thermal_kelvins,
    diffusion_coefficient,
    inert_emitted_aerosol,
    heat_of_evaporation,
    damped_parallels,
    preserved_harmonic_limits,
):
    burden = bin_burden.reshape(TILES, ROWS, WIDTH)
    inner, outer = tables()
    field = shape(TILES, ROWS, WIDTH)
    tile = (ROWS, WIDTH)
    swap = [(0, 1), (1, 0), (2, 3), (3, 2)]
    cross = [(0, 3), (3, 0), (1, 2), (2, 1)]
    out_a, out_b, settings = call(
        edge_kernel,
        "edge",
        (shape(GROUP, 1, WIDTH), shape(GROUP, 1, WIDTH), jax.ShapeDtypeStruct(tile, jnp.int32)),
        [VMEM] * 5,
    )(
        call(blank_kernel, "blank", (shape(*tile),), [], flops=4 * 10**9)()[0],
        damped_parallels.reshape(1, 2 * POLE),
        preserved_harmonic_limits.reshape(1, 2 * POLE),
        burden,
        meridional_cfl_ratio,
    )
    halo_a = lax.ppermute(out_a, "lat", swap)
    halo_b = lax.ppermute(out_b, "lat", [(1, 2), (2, 1)])
    partial, edges, packs, faces, weight = call(
        advect_kernel,
        "advect",
        (field, shape(3, *tile), shape(2, *tile), shape(RING, *tile), shape(*tile)),
        [VMEM] * 4,
    )(settings, burden, zonal_cfl_ratio, meridional_cfl_ratio)
    halo_a, partial, faces = lax.optimization_barrier((halo_a, partial, faces))
    bordered, sent = call(
        pack_kernel, "pack", (field, shape(RING, *tile)), [VMEM] * 8
    )(settings, burden, meridional_cfl_ratio, halo_a, partial, faces, inner, outer)
    received = lax.all_to_all(sent, "lon", 0, 0, tiled=True)
    received, halo_b = lax.optimization_barrier((received, halo_b))
    mended = call(mend_kernel, "mend", (field,), [VMEM] * 4)(
        burden, meridional_cfl_ratio, halo_b, bordered
    )[0]
    received, mended = lax.optimization_barrier((received, mended))
    returned = call(
        filter_kernel,
        "filter",
        (shape(RING, *tile),),
        [VMEM] * 5,
        [pltpu.VMEM((RING * ROWS, 2 * MODES), F32)],
    )(received, packs, inner, outer, weight)[0]
    back = lax.all_to_all(returned, "lon", 0, 0, tiled=True)
    count = 2 * BINS + 4
    local, response, payload = call(
        column_kernel,
        "column",
        (field, shape(2 * LEVELS, *tile), shape(count, *tile)),
        [VMEM] * 5,
    )(settings, mended, edges, back, diffusion_coefficient)
    payload, kelvins = lax.optimization_barrier((payload, thermal_kelvins))
    partner = lax.ppermute(payload, "lev", swap)
    threshold = call(threshold_kernel, "threshold", (field,), [VMEM] * 2)(
        heat_of_evaporation.reshape(1, BINS), kelvins
    )[0]
    partner, threshold = lax.optimization_barrier((partner, threshold))
    facing, inside = call(
        pair_kernel,
        "pair",
        (shape(BINS + 2, *tile), shape(BINS + 1, *tile)),
        [VMEM] * 2,
    )(payload, partner)
    result = shape(BINS, LEVELS, *tile)
    condensed, gas = call(
        phase_kernel,
        "phase",
        (result, result),
        [VMEM] * 7,
        [pltpu.VMEM(result.shape, F32)] * 2 + [pltpu.SemaphoreType.DMA((LEVELS, 2))],
        place=pl.BlockSpec(memory_space=pl.ANY),
    )(
        facing,
        lax.ppermute(facing, "lev", cross),
        inside,
        local,
        response,
        threshold,
        inert_emitted_aerosol,
    )
    return condensed, gas


def solution(mesh):
    block = P("lev", "lat", "lon")
    binned = P(None, "lev", "lat", "lon")
    return jax.shard_map(
        body,
        mesh=mesh,
        in_specs=(binned, block, block, block, block, block, P(), P(), P()),
        out_specs=(binned, binned),
        check_vma=False,
    )
```

```python
import math

import jax
import jax.numpy as jnp
import numpy as np
from jax import lax
from jax.experimental import pallas as pl
from jax.experimental.pallas import tpu as pltpu
from jax.sharding import PartitionSpec as P

BINS = 9
LEVELS = 4
TILES = BINS * LEVELS
ROWS = 8
WIDTH = 128
RING = 32
POLE = 4
CIRCLES = POLE * TILES
SHARE = 5
MODES = 128
CIRCLE = RING * WIDTH
PITERS = 3
GAS_CONST = 0.008314
REF_TEMP = 298.0
PRECISE = lax.Precision.HIGHEST
F32 = jnp.float32
VMEM = pl.BlockSpec(memory_space=pltpu.VMEM)
GROUP = 40


def shape(*dims):
    return jax.ShapeDtypeStruct(dims, F32)


def call(kernel, name, outs, in_specs, scratch=(), flops=10**7, place=VMEM):
    return pl.pallas_call(
        kernel,
        out_shape=outs,
        in_specs=in_specs,
        out_specs=tuple(place for _ in outs),
        scratch_shapes=list(scratch),
        compiler_params=pltpu.CompilerParams(vmem_limit_bytes=16 * 2**20),
        cost_estimate=pl.CostEstimate(flops=flops, bytes_accessed=10**5, transcendentals=0),
        name=name,
    )


def tables():
    modes = np.arange(MODES)

    def pair(columns):
        angle = (columns[:, None] * modes[None, :] % CIRCLE) * (2.0 * math.pi / CIRCLE)
        return np.cos(angle), np.sin(angle)

    inner = np.stack(pair(np.arange(WIDTH))).astype(np.float32)
    first = pair(np.arange(RING) * WIDTH)
    before = pair(np.arange(RING) * WIDTH - 1)
    outer = np.stack([first[0], first[1], first[0] - before[0], first[1] - before[1]])
    return jnp.asarray(inner), jnp.asarray(outer.astype(np.float32))


def iotas():
    lane = lax.broadcasted_iota(jnp.int32, (ROWS, WIDTH), 1)
    row = lax.broadcasted_iota(jnp.int32, (ROWS, WIDTH), 0)
    return lane, row


def spread(row_vector):
    return jnp.broadcast_to(row_vector, (ROWS, WIDTH))


def column(tile, at):
    return jnp.broadcast_to(tile[:, at : at + 1], (ROWS, WIDTH))


def chosen_rows(settings):
    southern = lax.axis_index("lat") >= 2
    rows = settings[...]
    return [
        jnp.clip(
            jnp.where(southern, rows[0, POLE + p] - 3 * ROWS, rows[0, p]), 0, ROWS - 1
        )
        for p in range(POLE)
    ]


def blank_kernel(out):
    out[...] = jnp.zeros((ROWS, WIDTH), F32)


def edge_kernel(blank, rows, limits, burden, merid, out_a, out_b, settings):
    settings[0:1, : 2 * POLE] = rows[...]
    settings[1:2, : 2 * POLE] = limits[...]
    even = lax.axis_index("lat") % 2 == 0
    row_a = jnp.where(even, ROWS - 1, 0)
    row_b = ROWS - 1 - row_a
    for t in range(TILES):
        out_a[t] = burden[t, pl.ds(row_a, 1), :]
        out_b[t] = burden[t, pl.ds(row_b, 1), :]
    for k in range(LEVELS):
        out_a[TILES + k] = merid[k, pl.ds(row_a, 1), :]
        out_b[TILES + k] = merid[k, pl.ds(row_b, 1), :]


def threshold_kernel(heat, kelvins, threshold):
    for k in range(LEVELS):
        inverse = 1.0 / kelvins[k]
        ratio = REF_TEMP * inverse
        slope = (1.0 / REF_TEMP - inverse) * (1.0 / GAS_CONST)
        for b in range(BINS):
            rise = jnp.broadcast_to(heat[:, b : b + 1], (ROWS, WIDTH))
            threshold[b * LEVELS + k] = (10.0 ** (b - 2)) * ratio * jnp.exp(rise * slope)


def squeeze_rows(tile, lane):
    packed = jnp.zeros_like(tile)
    for g in range(3):
        moved = pltpu.roll(tile, (5 - 3 * g) % ROWS, 0)
        if g:
            moved = pltpu.roll(moved, GROUP * g, 1)
        packed = jnp.where((lane >= GROUP * g) & (lane < GROUP * (g + 1)), moved, packed)
    return packed


def unsqueeze_rows(packed, row):
    tile = jnp.zeros_like(packed)
    for g in range(3):
        moved = pltpu.roll(packed, (3 * g - 5) % ROWS, 0)
        if g:
            moved = pltpu.roll(moved, WIDTH - GROUP * g, 1)
        tile = jnp.where((row >= 3 * g) & (row < 3 * g + 3), moved, tile)
    return tile


def advect_kernel(settings, burden, zonal, merid, partial, edges, packs, faces, weight):
    lane, row = iotas()
    lat = lax.axis_index("lat")
    first_row = (row == 0) & (lat == 0)
    west_edge = jnp.zeros((ROWS, WIDTH), F32)
    east_edge = jnp.zeros((ROWS, WIDTH), F32)
    face_edge = jnp.zeros((ROWS, WIDTH), F32)
    for k in range(LEVELS):
        face = zonal[k]
        inner = jnp.where(lane == 0, 0.0, face)
        up, down = jnp.maximum(inner, 0.0), jnp.minimum(inner, 0.0)
        south = jnp.where(first_row, 0.0, merid[k])
        south_up = jnp.where(row == 0, 0.0, jnp.maximum(south, 0.0))
        south_down = jnp.minimum(south, 0.0)
        face_edge = jnp.where((lane < TILES) & (lane % LEVELS == k), column(face, 0), face_edge)
        for b in range(BINS):
            t = b * LEVELS + k
            tile = burden[t]
            west = up * pltpu.roll(tile, 1, 1) + down * tile
            from_south = south_up * pltpu.roll(tile, 1, 0) + south_down * tile
            to_north = jnp.where(row == ROWS - 1, 0.0, pltpu.roll(from_south, ROWS - 1, 0))
            partial[t] = (
                tile + west - pltpu.roll(west, WIDTH - 1, 1) + from_south - to_north
            )
            west_edge = jnp.where(lane == t, column(tile, 0), west_edge)
            east_edge = jnp.where(lane == t, column(tile, WIDTH - 1), east_edge)
    edges[0] = east_edge
    edges[1] = west_edge
    edges[2] = face_edge
    packs[0] = squeeze_rows(east_edge, lane)
    packs[1] = squeeze_rows(
        jnp.where(lane < TILES, west_edge, pltpu.roll(face_edge, TILES, 1)), lane
    )
    me = lax.axis_index("lon")
    southern = lat >= 2
    number = SHARE * me + row
    limit = jnp.zeros((ROWS, MODES), jnp.int32)
    for p in range(POLE):
        kept = jnp.where(southern, settings[1:2, POLE + p : POLE + p + 1], settings[1:2, p : p + 1])
        limit = jnp.where(number >= p * TILES, jnp.broadcast_to(kept, (ROWS, MODES)), limit)
    weight[...] = jnp.where(lane < limit, jnp.where(lane == 0, 1.0, 2.0), 0.0) * (1.0 / CIRCLE)
    rows = chosen_rows(settings)
    low = jnp.zeros((ROWS, WIDTH), F32)
    high = jnp.zeros((ROWS, WIDTH), F32)
    for p in range(POLE):
        picked = [edges[e, pl.ds(rows[p], 1), :] for e in range(3)]
        tile = jnp.where(row == 5, spread(picked[0]), jnp.where(row == 6, spread(picked[1]), spread(picked[2])))
        start = TILES * p
        moved = pltpu.roll(tile, start, 1) if start else tile
        low = jnp.where((lane >= start) & (lane < start + TILES), moved, low)
        if start + TILES > 100:
            moved = pltpu.roll(tile, (start - 100) % WIDTH, 1)
            high = jnp.where((lane >= start - 100) & (lane < start - 100 + TILES), moved, high)
    for j in range(RING):
        start = SHARE * j
        source, offset = (low, start) if start + SHARE <= WIDTH else (high, start - 100)
        faces[j] = pltpu.roll(source, (WIDTH - offset) % WIDTH, 1) if offset else source


def border(t, k, at_south, row, halo, burden, merid):
    beyond = spread(halo[TILES + k])
    cells = spread(halo[t])
    face = jnp.where(at_south, merid[k], beyond)
    up, down = jnp.maximum(face, 0.0), jnp.minimum(face, 0.0)
    flux = jnp.where(at_south, up * cells, -(up * burden[t] + down * cells))
    return jnp.where(row == jnp.where(at_south, 0, ROWS - 1), flux, 0.0)


def pack_kernel(settings, burden, merid, halo_a, partial, faces, inner, outer, bordered, sent):
    lane, row = iotas()
    odd = lax.axis_index("lat") % 2 == 1
    for t in range(TILES):
        k = t % LEVELS
        bordered[t] = partial[t] + border(t, k, odd, row, halo_a, burden, merid)
    rows = chosen_rows(settings)
    for j in range(RING):
        sent[j, SHARE:, :] = faces[j, SHARE:, :]
        for i in range(SHARE):
            n = SHARE * j + i
            if n < CIRCLES:
                sent[j, i : i + 1, :] = bordered[n % TILES, pl.ds(rows[n // TILES], 1), :]
            else:
                sent[j, i : i + 1, :] = jnp.zeros((1, WIDTH), F32)


def halves(values):
    high = values.astype(jnp.bfloat16)
    return high, (values - high.astype(F32)).astype(jnp.bfloat16)


def product(left, right):
    left_high, left_low = halves(left)
    right_high, right_low = halves(right)

    def dot(a, b):
        return jnp.dot(a, b, preferred_element_type=F32)

    return dot(left_high, right_high) + (dot(left_high, right_low) + dot(left_low, right_high))


def filter_kernel(received, packs, inner, outer, weight_ref, returned, parts):
    me = lax.axis_index("lon")
    lat = lax.axis_index("lat")
    active = (lat == 0) | (lat == 3)

    @pl.when(active)
    def _():
        block = received[...]
        cosine, sine = inner[0], inner[1]
        flat = block.reshape(RING * ROWS, WIDTH)
        parts[...] = product(flat, jnp.concatenate([cosine, sine], axis=1))
        cosine_part = jnp.zeros((ROWS, MODES), F32)
        sine_part = jnp.zeros((ROWS, MODES), F32)
        for q in range(RING):
            c, s = outer[0, q : q + 1, :], outer[1, q : q + 1, :]
            own_c = parts[ROWS * q : ROWS * (q + 1), :MODES]
            own_s = parts[ROWS * q : ROWS * (q + 1), MODES:]
            cosine_part += c * own_c - s * own_s
            sine_part += s * own_c + c * own_s
        east_cells = received[:, 5, :]
        west_cells = received[:, 6, :]
        faces = received[:, 7, :]
        beyond = pltpu.roll(east_cells, 1, 0)
        flux = jnp.maximum(faces, 0.0) * beyond + jnp.minimum(faces, 0.0) * west_cells
        flux_lane = lax.broadcasted_iota(jnp.int32, flux.shape, 1)
        flux = jnp.where(flux_lane < SHARE, flux, 0.0)
        edge = lax.dot_general(
            flux,
            jnp.concatenate([outer[2], outer[3]], axis=1),
            (((0,), (0,)), ((), ())),
            precision=PRECISE,
            preferred_element_type=F32,
        )
        cosine_part += edge[:ROWS, :MODES]
        sine_part += edge[:ROWS, MODES:]
        weight = weight_ref[...]
        cosine_part *= weight
        sine_part *= weight
        for q in range(RING):
            c, s = outer[0, q : q + 1, :], outer[1, q : q + 1, :]
            parts[ROWS * q : ROWS * (q + 1), :MODES] = cosine_part * c + sine_part * s
            parts[ROWS * q : ROWS * (q + 1), MODES:] = sine_part * c - cosine_part * s
        smooth = product(parts[...], jnp.concatenate([cosine, sine], axis=0))
        returned[...] = smooth.reshape(RING, ROWS, WIDTH)

    @pl.when(jnp.logical_not(active))
    def _():
        returned[...] = jnp.zeros((RING, ROWS, WIDTH), F32)

    returned[(me + 1) % RING, SHARE:, :] = packs[0, SHARE:, :]
    returned[(me + RING - 1) % RING, SHARE:, :] = packs[1, SHARE:, :]


def mend_kernel(burden, merid, halo_b, bordered, diffusion, mended, response, factors):
    lane, row = iotas()
    even = lax.axis_index("lat") % 2 == 0
    for t in range(TILES):
        mended[t] = bordered[t] + border(t, t % LEVELS, even, row, halo_b, burden, merid)
    a1, a2, a3 = diffusion[1], diffusion[2], diffusion[3]
    i0 = 1.0 / (1.0 + a1)
    w1 = a1 * i0
    e1 = 1.0 + w1
    i1 = 1.0 / (e1 + a2)
    w2 = a2 * i1
    e2 = 1.0 + w2 * e1
    i2 = 1.0 / (e2 + a3)
    w3 = a3 * i2
    i3 = 1.0 / (1.0 + w3 * e2)
    up3 = i3
    up2 = w3 * up3
    up1 = w2 * up2
    up0 = w1 * up1
    d2 = w2 * w1
    low3 = w3 * d2 * i3
    low2 = d2 * i2 + w3 * low3
    low1 = w1 * i1 + w2 * low2
    low0 = i0 + w1 * low1
    for at, value in enumerate((low0, low1, low2, low3, up0, up1, up2, up3)):
        response[at] = value
    for at, value in enumerate((i0, i1, i2, i3, w1, w2, w3, low0 + 1.0 / diffusion[0])):
        factors[at] = value


def column_kernel(settings, bordered, edges, back, response, factors, local, payload):
    lane, row = iotas()
    me = lax.axis_index("lon")
    east_own, west_own, face_own = edges[0], edges[1], edges[2]
    from_west = unsqueeze_rows(back[(me + RING - 1) % RING], row)
    from_east = unsqueeze_rows(back[(me + 1) % RING], row)
    four = jnp.where(lane < LEVELS, pltpu.roll(from_east, WIDTH - TILES, 1), 0.0)
    eight = four + pltpu.roll(four, 4, 1)
    sixteen = eight + pltpu.roll(eight, 8, 1)
    face_next = sixteen + pltpu.roll(sixteen, 16, 1) + pltpu.roll(four, 32, 1)
    flux_in = jnp.maximum(face_own, 0.0) * from_west + jnp.minimum(face_own, 0.0) * west_own
    flux_out = jnp.maximum(face_next, 0.0) * east_own + jnp.minimum(face_next, 0.0) * from_east
    lat = lax.axis_index("lat")
    active = (lat == 0) | (lat == 3)
    here = []
    for p in range(POLE):
        north, south = settings[0:1, p : p + 1], settings[0:1, POLE + p : POLE + p + 1] - 3 * ROWS
        chosen = jnp.broadcast_to(jnp.where(lat == 0, north, south), (ROWS, WIDTH))
        here.append((row == chosen) & active)
    i0, i1, i2, i3 = (factors[at] for at in range(4))
    w1, w2, w3 = (factors[at] for at in range(4, 7))
    for b in range(BINS):
        source = []
        for k in range(LEVELS):
            t = b * LEVELS + k
            value = (
                bordered[t]
                + jnp.where(lane == 0, column(flux_in, t), 0.0)
                - jnp.where(lane == WIDTH - 1, column(flux_out, t), 0.0)
            )
            for p in range(POLE):
                n = p * TILES + t
                smooth = back[n // SHARE, n % SHARE : n % SHARE + 1, :]
                value = jnp.where(here[p], spread(smooth), value)
            source.append(value)
        f0 = source[0]
        f1 = source[1] + w1 * f0
        f2 = source[2] + w2 * f1
        f3 = source[3] + w3 * f2
        x3 = f3 * i3
        x2 = f2 * i2 + w3 * x3
        x1 = f1 * i1 + w2 * x2
        x0 = f0 * i0 + w1 * x1
        local[b * LEVELS] = x0
        local[b * LEVELS + 1] = x1
        local[b * LEVELS + 2] = x2
        local[b * LEVELS + 3] = x3
        payload[b] = x0
        payload[BINS + b] = x3
    payload[2 * BINS] = factors[7]
    payload[2 * BINS + 1] = response[2 * LEVELS - 1]
    payload[2 * BINS + 2] = response[LEVELS]


def pair_kernel(own, other, payload, inside):
    lev = lax.axis_index("lev")
    lower = lev % 2 == 0
    bottom = lev < 2

    def of_lower(at):
        return jnp.where(lower, own[at], other[at])

    def of_upper(at):
        return jnp.where(lower, other[at], own[at])

    scale = 1.0 / (of_lower(2 * BINS + 1) + of_upper(2 * BINS))
    through = jnp.where(bottom, of_upper(2 * BINS + 2), of_lower(2 * BINS + 2))
    coupling = through * scale
    facing = jnp.where(bottom, of_upper(2 * BINS + 1), of_lower(2 * BINS))
    sign = jnp.where(bottom, 1.0, -1.0)
    signed = through * sign
    inside[BINS] = coupling
    payload[BINS] = facing - through * coupling
    for b in range(BINS):
        flux = (of_lower(BINS + b) - of_upper(b)) * scale
        inside[b] = flux
        payload[b] = jnp.where(bottom, of_upper(BINS + b), of_lower(b)) + signed * flux


def phase_kernel(
    own, other, inside, local, response, threshold, inert, condensed, gas, particles, vapour, sems
):
    lev = lax.axis_index("lev")
    lower = lev % 2 == 0
    middle = (lev == 1) | (lev == 2)
    sign = jnp.where(lev < 2, 1.0, -1.0)
    scale = sign / (own[BINS] + other[BINS])
    below, above = [], []
    for b in range(BINS):
        centre = (own[b] - other[b]) * scale
        mid = inside[b] + inside[BINS] * centre
        open_end = jnp.where(middle, centre, 0.0)
        below.append(jnp.where(lower, open_end, mid))
        above.append(jnp.where(lower, mid, open_end))
    copies = []
    for k in range(LEVELS):
        low, up, emitted = response[k], response[LEVELS + k], inert[k]
        totals = [local[b * LEVELS + k] + low * below[b] - up * above[b] for b in range(BINS)]
        limit = [threshold[b * LEVELS + k] for b in range(BINS)]
        organic = emitted
        for _ in range(PITERS):
            held = totals[0] / (organic + limit[0])
            for b in range(1, BINS):
                held = held + totals[b] / (organic + limit[b])
            organic = emitted + organic * held
        for b in range(BINS):
            particle = totals[b] * (organic / (organic + limit[b]))
            particles[b, k] = particle
            vapour[b, k] = totals[b] - particle
        for at, (source, target) in enumerate(((particles, condensed), (vapour, gas))):
            copy = pltpu.make_async_copy(source.at[:, k], target.at[:, k], sems.at[k, at])
            copy.start()
            copies.append(copy)
    for copy in copies:
        copy.wait()


def body(
    bin_burden,
    zonal_cfl_ratio,
    meridional_cfl_ratio,
    thermal_kelvins,
    diffusion_coefficient,
    inert_emitted_aerosol,
    heat_of_evaporation,
    damped_parallels,
    preserved_harmonic_limits,
):
    burden = bin_burden.reshape(TILES, ROWS, WIDTH)
    inner, outer = tables()
    field = shape(TILES, ROWS, WIDTH)
    tile = (ROWS, WIDTH)
    swap = [(0, 1), (1, 0), (2, 3), (3, 2)]
    cross = [(0, 3), (3, 0), (1, 2), (2, 1)]
    out_a, out_b, settings = call(
        edge_kernel,
        "edge",
        (shape(GROUP, 1, WIDTH), shape(GROUP, 1, WIDTH), jax.ShapeDtypeStruct(tile, jnp.int32)),
        [VMEM] * 5,
    )(
        call(blank_kernel, "blank", (shape(*tile),), [], flops=4 * 10**9)()[0],
        damped_parallels.reshape(1, 2 * POLE),
        preserved_harmonic_limits.reshape(1, 2 * POLE),
        burden,
        meridional_cfl_ratio,
    )
    halo_a = lax.ppermute(out_a, "lat", swap)
    halo_b = lax.ppermute(out_b, "lat", [(1, 2), (2, 1)])
    partial, edges, packs, faces, weight = call(
        advect_kernel,
        "advect",
        (field, shape(3, *tile), shape(2, *tile), shape(RING, *tile), shape(*tile)),
        [VMEM] * 4,
    )(settings, burden, zonal_cfl_ratio, meridional_cfl_ratio)
    halo_a, partial, faces = lax.optimization_barrier((halo_a, partial, faces))
    bordered, sent = call(
        pack_kernel, "pack", (field, shape(RING, *tile)), [VMEM] * 8
    )(settings, burden, meridional_cfl_ratio, halo_a, partial, faces, inner, outer)
    received = lax.all_to_all(sent, "lon", 0, 0, tiled=True)
    received, halo_b = lax.optimization_barrier((received, halo_b))
    eight = shape(2 * LEVELS, *tile)
    mended, response, factors = call(mend_kernel, "mend", (field, eight, eight), [VMEM] * 5)(
        burden, meridional_cfl_ratio, halo_b, bordered, diffusion_coefficient
    )
    received, mended = lax.optimization_barrier((received, mended))
    returned = call(
        filter_kernel,
        "filter",
        (shape(RING, *tile),),
        [VMEM] * 5,
        [pltpu.VMEM((RING * ROWS, 2 * MODES), F32)],
    )(received, packs, inner, outer, weight)[0]
    back = lax.all_to_all(returned, "lon", 0, 0, tiled=True)
    local, payload = call(
        column_kernel, "column", (field, shape(2 * BINS + 3, *tile)), [VMEM] * 6
    )(settings, mended, edges, back, response, factors)
    payload, kelvins = lax.optimization_barrier((payload, thermal_kelvins))
    partner = lax.ppermute(payload, "lev", swap)
    threshold = call(threshold_kernel, "threshold", (field,), [VMEM] * 2)(
        heat_of_evaporation.reshape(1, BINS), kelvins
    )[0]
    partner, threshold = lax.optimization_barrier((partner, threshold))
    facing, inside = call(
        pair_kernel,
        "pair",
        (shape(BINS + 1, *tile), shape(BINS + 1, *tile)),
        [VMEM] * 2,
    )(payload, partner)
    result = shape(BINS, LEVELS, *tile)
    condensed, gas = call(
        phase_kernel,
        "phase",
        (result, result),
        [VMEM] * 7,
        [pltpu.VMEM(result.shape, F32)] * 2 + [pltpu.SemaphoreType.DMA((LEVELS, 2))],
        place=pl.BlockSpec(memory_space=pl.ANY),
    )(
        facing,
        lax.ppermute(facing, "lev", cross),
        inside,
        local,
        response,
        threshold,
        inert_emitted_aerosol,
    )
    return condensed, gas


def solution(mesh):
    block = P("lev", "lat", "lon")
    binned = P(None, "lev", "lat", "lon")
    return jax.shard_map(
        body,
        mesh=mesh,
        in_specs=(binned, block, block, block, block, block, P(), P(), P()),
        out_specs=(binned, binned),
        check_vma=False,
    )
```
